256 devices in a mesh: inst: 32 (over x, y, core), head: 8 (over z).
Axes of the slice: x: 4, y: 4, z: 8, core: 2. Of those that a mesh axis runs over, the one named last changes fastest.
Arguments:
- query: bfloat16 [2, 8, 64, 128], P(None, None, 'head')
- new_keys: bfloat16 [2, 8, 8, 128], P(None, None, 'head'), as said below
- new_values: bfloat16 [2, 8, 8, 128], P(None, None, 'head'), may hold values from -24 to 24
- cache_keys: bfloat16 [2048, 128, 8, 128], P('inst', None, 'head'), as said below
- cache_values: bfloat16 [2048, 128, 8, 128], P('inst', None, 'head'), may hold values from -24 to 24
- signs: int32 [8, 128], P('head'), may hold values from 0 to 1
- block_req: int32 [2048], replicated, may hold values from 0 to 7, as said below
- block_fill: int32 [2048], replicated, may hold values from 1 to 128, as said below
- dest_inst: int32 [2048], replicated, may hold values from 0 to 31, as said below
- new_slot: int32 [2048], replicated, may hold values from 0 to 63, as said below
- out_weight: bfloat16 [8192, 8192], P('head', 'inst'), may hold values from -0.125 to 0.125
Outputs:
- layer_out: bfloat16 [2, 8, 8192], P(None, None, 'inst')
- moved_keys: bfloat16 [2048, 128, 8, 128], P('inst', None, 'head')
- moved_values: bfloat16 [2048, 128, 8, 128], P('inst', None, 'head')
The draws below stay inside these ranges and needn't reach their ends.
Inputs may be any that keep to these rules, and one draw needn't show every extreme that they name: `new_keys`: keys of the new tokens. `cache_keys`: rotated cached keys; positions at or after a block's fill hold stale entries. `block_req`: every request holds two blocks or more. `block_fill`: one block of each request may be partly live; all its other blocks hold 128 live positions. `dest_inst`: half of the instances are released: each of them sends exactly 4 of its blocks to every kept instance and keeps none; every kept instance keeps all its own blocks; the first and the last instance are always kept. `new_slot`: for a moved block its row among the 64 rows of its new instance, every row of a kept instance taken by exactly one moved block; for a block that stays, its own slot on its instance.
All inputs are finite; a program needn't handle non-finite values.
Results may differ from the reference program's by a relative error of at most 0.02.
Values may be sent and summed in bfloat16 or wider, within the bound.
A program may use at most 64 MiB of HBM per device.

```python
import math
import jax
import jax.numpy as jnp
from jax import lax

D = 8192
QH = 64
KVH = 8
HD = 128
REQS = 8
STEPS = 2
BT = 128
SLOTS = 64
GROUP = 8
NB = 2048
N_INST = 32


def sign_bits(key):
    return jax.random.randint(jax.random.fold_in(key, 404), (KVH, HD), 0, 2).astype(jnp.int32)


def plan_tables(key):
    plan_key = jax.random.fold_in(key, 101)
    middle_order = jax.random.permutation(jax.random.fold_in(plan_key, 1), N_INST - 2).astype(jnp.int32) + 1
    inst_order = jnp.concatenate([jnp.array([N_INST - 1, 0], jnp.int32), middle_order]).astype(jnp.int32)
    position = jnp.argsort(inst_order).astype(jnp.int32)
    keep_count = N_INST // 2
    pair_count = SLOTS // keep_count
    slot_ids = jnp.arange(SLOTS, dtype=jnp.int32)
    send_draw = jax.random.randint(jax.random.fold_in(plan_key, 2), (N_INST, SLOTS), 0, 65536) * SLOTS + slot_ids[None, :]
    send_rank = jnp.argsort(jnp.argsort(send_draw, axis=1), axis=1).astype(jnp.int32)
    recv_draw = jax.random.randint(jax.random.fold_in(plan_key, 3), (N_INST, SLOTS), 0, 65536) * SLOTS + slot_ids[None, :]
    recv_perm = jnp.argsort(recv_draw, axis=1).astype(jnp.int32)
    inst_ids = jnp.arange(N_INST, dtype=jnp.int32)[:, None]
    inst_position = position[inst_ids]
    released = inst_position >= keep_count
    run_index = send_rank // pair_count
    dest_position = (inst_position - keep_count + run_index) % keep_count
    dest_rows = jnp.where(released, inst_order[dest_position], inst_ids + 0 * slot_ids[None, :])
    slot_rows = jnp.where(released, recv_perm[dest_rows, send_rank], slot_ids[None, :] + 0 * inst_ids)
    return (dest_rows.reshape(-1).astype(jnp.int32), slot_rows.reshape(-1).astype(jnp.int32))


def request_layout(key):
    req_key = jax.random.fold_in(key, 202)
    block_count = SLOTS * N_INST
    req_ids = jnp.arange(REQS, dtype=jnp.int32)
    weights = jax.random.randint(jax.random.fold_in(req_key, 1), (REQS,), 1, 9)
    spare_blocks = block_count - 2 * REQS
    per_request = 2 + weights * spare_blocks // jnp.sum(weights)
    per_request = per_request + jnp.where(req_ids == 0, block_count - jnp.sum(per_request), 0)
    block_ends = jnp.cumsum(per_request).astype(jnp.int32)
    shuffled = jax.random.permutation(jax.random.fold_in(req_key, 2), block_count).astype(jnp.int32)
    return (shuffled, block_ends)


def request_tables(key):
    shuffled, block_ends = request_layout(key)
    req_key = jax.random.fold_in(key, 202)
    block_count = SLOTS * N_INST
    request_rows = jnp.sum((shuffled[:, None] >= block_ends[None, :]).astype(jnp.int32), axis=1)
    last_block = shuffled == block_ends[request_rows] - 1
    partial_fill = jax.random.randint(jax.random.fold_in(req_key, 3), (block_count,), 1, BT + 1)
    fill_rows = jnp.where(last_block, partial_fill, BT)
    return (request_rows.astype(jnp.int32), fill_rows.astype(jnp.int32))


def draw_dest_inst(key, part):
    dest_rows, slot_rows = plan_tables(key)
    return dest_rows


def draw_new_slot(key, part):
    dest_rows, slot_rows = plan_tables(key)
    return slot_rows


def draw_block_req(key, part):
    request_rows, fill_rows = request_tables(key)
    return request_rows


def draw_block_fill(key, part):
    request_rows, fill_rows = request_tables(key)
    return fill_rows


def draw_signs(key, part):
    bit_rows = sign_bits(key)
    return bit_rows


def draw_cache_keys(key, part):
    request_rows, fill_rows = request_tables(key)
    key = jax.random.fold_in(key, 15)
    block_count = SLOTS * N_INST
    live_mask = jnp.arange(BT, dtype=jnp.int32)[None, :] < fill_rows[:, None]
    stale_scale = jnp.where(live_mask, 1.0, 4.0).astype(jnp.float32)[:, :, None, None]
    shape_full = (block_count, BT, KVH, HD)
    base_draw = jax.random.normal(jax.random.fold_in(key, 1), shape_full, jnp.float32)
    token_scale = jnp.exp(jax.random.uniform(jax.random.fold_in(key, 2), (block_count, BT, KVH, 1), jnp.float32, math.log(0.25), math.log(2.5)))
    channel_scale = jnp.exp(jax.random.uniform(jax.random.fold_in(key, 3), (1, 1, KVH, HD), jnp.float32, math.log(0.3), math.log(3.0)))
    return (base_draw * token_scale * channel_scale * stale_scale).astype(jnp.bfloat16)


def draw_query(key, part):
    key = jax.random.fold_in(key, 16)
    return jax.random.normal(key, (STEPS, REQS, QH, HD), jnp.float32).astype(jnp.bfloat16)


def draw_new_keys(key, part):
    key = jax.random.fold_in(key, 17)
    return (4.0 * jax.random.normal(key, (STEPS, REQS, KVH, HD), jnp.float32)).astype(jnp.bfloat16)


def strengthened(values, own_key, source, target, parts, factor):
    def block_of(dim):
        return (jnp.arange(values.shape[dim]) // (values.shape[dim] // parts)).reshape((-1,) + (1,) * (values.ndim - 1 - dim))

    one_side = jax.random.permutation(own_key, parts)[block_of(target)]
    far = (block_of(target) + parts // 2) % parts
    return jnp.where((block_of(source) == one_side) | (block_of(source) == far), factor * values, values)


def block_levels(key, extent, split, smallest, largest):
    def one(dim, blocks):
        steps = jax.random.uniform(jax.random.fold_in(jax.random.fold_in(key, 6), dim), (blocks,), jnp.float32, smallest / len(split), largest / len(split))
        return jnp.repeat(jnp.exp(steps), extent[dim] // blocks).reshape((-1,) + (1,) * (len(extent) - dim - 1))

    loudness = one(*split[0])
    for cut in split[1:]:
        loudness = loudness * one(*cut)
    return loudness


def gaussian(key, shape, spread, reach, cuts=(), kind=jnp.bfloat16):
    drawn = spread * jax.random.normal(key, shape, jnp.float32)
    if cuts:
        drawn = drawn * block_levels(key, shape, cuts, -0.22, 0.18)
    return jnp.clip(drawn, -reach, reach).astype(kind)


def heavy_noise(rng, shape, spread, most, cuts, heavy, kind=jnp.bfloat16):
    values = spread * jax.random.normal(rng, shape, jnp.float32)
    if cuts:
        values = values * block_levels(rng, shape, cuts, -0.22, 0.18)
    return jnp.clip(strengthened(values, jax.random.fold_in(rng, 3), *heavy), -most, most).astype(kind)


def setup_inputs(seed: int = 0) -> dict:
    key_of = jax.random.split(jax.random.key(seed), 12)
    query = draw_query(jax.random.fold_in(key_of[11], 71), 0)
    new_keys = draw_new_keys(jax.random.fold_in(key_of[11], 71), 0)
    new_values = gaussian(key_of[2], (STEPS, REQS, KVH, HD), 4.0, 24.0, ((2, 8),))
    cache_keys = draw_cache_keys(jax.random.fold_in(key_of[11], 71), 0)
    cache_values = gaussian(key_of[4], (NB, BT, KVH, HD), 4.0, 24.0, ((0, 32), (2, 8)))
    signs = draw_signs(jax.random.fold_in(key_of[11], 71), 0)
    block_req = draw_block_req(jax.random.fold_in(key_of[11], 71), 0)
    block_fill = draw_block_fill(jax.random.fold_in(key_of[11], 71), 0)
    dest_inst = draw_dest_inst(jax.random.fold_in(key_of[11], 71), 0)
    new_slot = draw_new_slot(jax.random.fold_in(key_of[11], 71), 0)
    out_weight = heavy_noise(key_of[10], (QH * HD, D), (QH * HD) ** -0.5, 0.125, ((0, 8), (1, 32)), (0, 1, 32, 2.75))
    return {"query": query, "new_keys": new_keys, "new_values": new_values, "cache_keys": cache_keys, "cache_values": cache_values, "signs": signs, "block_req": block_req, "block_fill": block_fill, "dest_inst": dest_inst, "new_slot": new_slot, "out_weight": out_weight}


NEG_FILL = -1e+30
HIGHEST = lax.Precision.HIGHEST

def hadamard_matrix(order_size):
    index_row = jnp.arange(order_size, dtype=jnp.int32)
    common = jnp.bitwise_and(index_row[:, None], index_row[None, :])
    parity = jnp.zeros((order_size, order_size), jnp.int32)
    for bit_index in range(order_size.bit_length() - 1):
        parity = parity + jnp.bitwise_and(jnp.right_shift(common, bit_index), 1)
    return (1 - 2 * jnp.bitwise_and(parity, 1)).astype(jnp.float32)

def rotation_tables(signs, order_size):
    sign_values = (2 * signs - 1).astype(jnp.float32)
    return sign_values[:, :, None] * hadamard_matrix(order_size)[None, :, :] / math.sqrt(order_size)

def cache_partial(q_low, cache_keys, cache_values, block_req, block_fill, score_scale):
    token_req = jnp.broadcast_to(block_req[:, None], (block_req.shape[0], BT)).reshape(-1)
    positions = jnp.arange(BT, dtype=jnp.int32)
    token_live = (positions[None, :] < block_fill[:, None]).reshape(-1)
    requests = jnp.arange(REQS, dtype=jnp.int32)
    live_mask = (token_req[None, :] == requests[:, None]) & token_live[None, :]
    live_full = live_mask[None, :, None, :]

    def one_head(head_index):
        key_rows = lax.dynamic_index_in_dim(cache_keys, head_index, 2, keepdims=False).reshape(-1, HD).astype(jnp.float32)
        value_rows = lax.dynamic_index_in_dim(cache_values, head_index, 2, keepdims=False).reshape(-1, HD).astype(jnp.float32)
        q_head = lax.dynamic_index_in_dim(q_low, head_index, 2, keepdims=False).astype(jnp.float32)
        scores = jnp.einsum('srgd,td->srgt', q_head, key_rows, precision=HIGHEST) * score_scale
        masked = jnp.where(live_full, scores, NEG_FILL)
        head_max = lax.optimization_barrier(jnp.max(masked, axis=-1))
        exp_terms = jnp.where(live_full, jnp.exp(masked - head_max[..., None]), 0.0)
        head_total = lax.optimization_barrier(jnp.sum(exp_terms, axis=-1))
        weights_low = lax.optimization_barrier(exp_terms.astype(jnp.bfloat16)).astype(jnp.float32)
        head_sum = jnp.einsum('srgt,td->srgd', weights_low, value_rows, precision=HIGHEST)
        return (head_max, head_total, head_sum)
    maxima, totals, sums = lax.map(one_head, jnp.arange(KVH, dtype=jnp.int32))
    return (jnp.moveaxis(maxima, 0, 2), jnp.moveaxis(totals, 0, 2), jnp.moveaxis(sums, 0, 2))

def reference(query, new_keys, new_values, cache_keys, cache_values, signs, block_req, block_fill, dest_inst, new_slot, out_weight):
    score_scale = 1.0 / math.sqrt(HD)
    rotation = rotation_tables(signs, HD)
    query_f = query.astype(jnp.float32).reshape(STEPS, REQS, KVH, GROUP, HD)
    q_rot = jnp.einsum('srkgi,kij->srkgj', query_f, rotation, precision=HIGHEST)
    q_low = lax.optimization_barrier(q_rot.astype(jnp.bfloat16))
    cache_max, cache_total, cache_sum = cache_partial(q_low, cache_keys, cache_values, block_req, block_fill, score_scale)
    new_rot = jnp.einsum('srki,kij->srkj', new_keys.astype(jnp.float32), rotation, precision=HIGHEST)
    value_rot = jnp.einsum('srki,kij->srkj', new_values.astype(jnp.float32), rotation, precision=HIGHEST)
    new_scores = jnp.einsum('srkgd,jrkd->srkgj', q_rot, new_rot, precision=HIGHEST) * score_scale
    step_ids = jnp.arange(STEPS, dtype=jnp.int32)
    causal = (step_ids[None, :] <= step_ids[:, None])[:, None, None, None, :]
    new_scores = jnp.where(causal, new_scores, NEG_FILL)
    joined_max = jnp.maximum(cache_max, lax.optimization_barrier(jnp.max(new_scores, axis=-1)))
    cache_factor = jnp.exp(cache_max - joined_max)
    new_weights = jnp.where(causal, jnp.exp(new_scores - joined_max[..., None]), 0.0)
    denominator = cache_factor * cache_total + lax.optimization_barrier(jnp.sum(new_weights, axis=-1))
    numerator = cache_factor[..., None] * cache_sum + jnp.einsum('srkgj,jrkd->srkgd', new_weights, value_rot, precision=HIGHEST)
    attended_rot = numerator / denominator[..., None]
    attended = jnp.einsum('srkgj,kij->srkgi', attended_rot, rotation, precision=HIGHEST).astype(jnp.bfloat16)
    flat_rows = attended.reshape(STEPS * REQS, QH * HD)
    layer_out = jnp.dot(flat_rows, out_weight, preferred_element_type=jnp.float32).astype(jnp.bfloat16).reshape(STEPS, REQS, D)
    source = jnp.arange(NB, dtype=jnp.int32) // SLOTS
    moved_mask = dest_inst != source
    target = jnp.where(moved_mask, dest_inst * SLOTS + new_slot, NB).astype(jnp.int32)
    moved_keys = jnp.zeros_like(cache_keys).at[target].set(cache_keys, mode='drop')
    moved_values = jnp.zeros_like(cache_values).at[target].set(cache_values, mode='drop')
    return (layer_out, moved_keys, moved_values)
```

```python
import functools
import math

import jax
import jax.numpy as jnp
from jax import lax
from jax.experimental import pallas as pl
from jax.experimental.pallas import tpu as pltpu
from jax.sharding import PartitionSpec as P

NEG_FILL = -1e30
HIGHEST = lax.Precision.HIGHEST
MESH = pl.DeviceIdType.MESH
INST = 32
HEADS = 8
PER = 4
SLOTS = 64
BT = 128
HD = 128
ROWS = 128
CHUNK = 4


def hadamard(order_size):
    common = jnp.bitwise_and(
        lax.broadcasted_iota(jnp.int32, (order_size, order_size), 0),
        lax.broadcasted_iota(jnp.int32, (order_size, order_size), 1),
    )
    parity = common
    for shift in (4, 2, 1):
        parity = jnp.bitwise_xor(parity, jnp.right_shift(parity, shift))
    return (1 - 2 * jnp.bitwise_and(parity, 1)).astype(jnp.float32)


def remote(src, dst, send_sem, recv_sem, inst, head):
    return pltpu.make_async_remote_copy(
        src_ref=src,
        dst_ref=dst,
        send_sem=send_sem,
        recv_sem=recv_sem,
        device_id=(inst, head),
        device_id_type=MESH,
    )


def attend(plan_ref, q_low, kc, vc, scores, scale):
    row_req = lax.broadcasted_iota(jnp.int32, (ROWS, BT), 0) // 8 % 8
    token = lax.broadcasted_iota(jnp.int32, (ROWS, BT), 1)
    chunks = SLOTS // CHUNK

    def score_chunk(i, top):
        keys = kc[pl.ds(i * CHUNK, CHUNK)].reshape(CHUNK * BT, HD)
        s = lax.dot_general(
            q_low, keys, (((1,), (1,)), ((), ())), preferred_element_type=jnp.float32
        )
        for c in range(CHUNK):
            req = plan_ref[128 + i * CHUNK + c]
            fill = plan_ref[192 + i * CHUNK + c]
            live = (row_req == req) & (token < fill)
            part = jnp.where(live, s[:, c * BT : (c + 1) * BT] * scale, NEG_FILL)
            scores[i, :, c * BT : (c + 1) * BT] = part
            top = jnp.maximum(top, part)
        return top

    top = lax.fori_loop(0, chunks, score_chunk, jnp.full((ROWS, BT), NEG_FILL, jnp.float32))
    row_max = jnp.max(top, axis=1, keepdims=True)

    def value_chunk(i, carry):
        total, acc = carry
        p = jnp.exp(scores[i] - row_max)
        for c in range(CHUNK):
            total = total + p[:, c * BT : (c + 1) * BT]
        values = vc[pl.ds(i * CHUNK, CHUNK)].reshape(CHUNK * BT, HD)
        acc = acc + jnp.dot(p.astype(jnp.bfloat16), values, preferred_element_type=jnp.float32)
        return total, acc

    zero = jnp.zeros((ROWS, BT), jnp.float32)
    total, acc = lax.fori_loop(0, chunks, value_chunk, (zero, zero))
    return row_max, jnp.sum(total, axis=1, keepdims=True), acc


def finish_rows(parts, group, q_group, nk, nv, sign_row, rotate, scale):
    req, step = group % 8, group // 8
    part_max = parts[:, :, HD : HD + 1]
    part_total = parts[:, :, HD + 64 : HD + 65]
    cache_max = jnp.max(part_max, axis=0)
    factor = jnp.exp(part_max - cache_max[None])
    cache_total = jnp.sum(part_total * factor, axis=0)
    cache_sum = jnp.sum(parts[:, :, :HD] * factor, axis=0)
    new_scores = (
        lax.dot_general(q_group, nk, (((1,), (1,)), ((), ())), preferred_element_type=jnp.float32)
        * scale
    )
    col = lax.broadcasted_iota(jnp.int32, (8, 16), 1)
    causal = (col % 8 == req) & (col // 8 <= step)
    new_scores = jnp.where(causal, new_scores, NEG_FILL)
    joined_max = jnp.maximum(cache_max, jnp.max(new_scores, axis=1, keepdims=True))
    cache_factor = jnp.exp(cache_max - joined_max)
    weights = jnp.where(causal, jnp.exp(new_scores - joined_max), 0.0)
    denominator = cache_factor * cache_total + jnp.sum(weights, axis=1, keepdims=True)
    back = jnp.dot(
        cache_factor * cache_sum, rotate, precision=HIGHEST, preferred_element_type=jnp.float32
    )
    back = back * sign_row * (1.0 / math.sqrt(HD))
    fresh = jnp.dot(weights, nv, precision=HIGHEST, preferred_element_type=jnp.float32)
    return (back + fresh) / denominator


def layer_kernel(
    plan_ref,
    q_ref,
    nk_ref,
    nv_ref,
    signs_ref,
    w_ref,
    ck_ref,
    cv_ref,
    out_ref,
    rk_ref,
    rv_ref,
    kc,
    vc,
    sk,
    sv,
    scores,
    qf,
    part_send,
    part_recv,
    att,
    proj,
    load_sem,
    k_send,
    k_recv,
    v_send,
    v_recv,
    part_s,
    part_r,
    att_s,
    att_r,
    proj_s,
    proj_r,
):
    me = lax.axis_index("inst")
    head = lax.axis_index("head")
    chip, core = me // 2, me % 2
    scale = 1.0 / math.sqrt(HD)

    load_k = pltpu.make_async_copy(ck_ref, kc, load_sem.at[0])
    load_v = pltpu.make_async_copy(cv_ref, vc, load_sem.at[1])
    load_k.start()
    load_v.start()

    barrier = pltpu.get_barrier_semaphore()

    def greet_inst(o, _):
        pl.semaphore_signal(
            barrier, inc=1, device_id=(lax.rem(me + o, INST), head), device_id_type=MESH
        )
        return 0

    def greet_head(o, _):
        pl.semaphore_signal(
            barrier, inc=1, device_id=(me, lax.rem(head + o, HEADS)), device_id_type=MESH
        )
        return 0

    lax.fori_loop(1, INST, greet_inst, 0)
    lax.fori_loop(1, HEADS, greet_head, 0)

    sign_row = (2 * signs_ref[...] - 1).astype(jnp.float32)
    rotate = hadamard(HD)
    raw = q_ref[...].astype(jnp.float32)
    qf[...] = raw
    q_rot = jnp.dot(
        (raw * sign_row).astype(jnp.bfloat16),
        rotate.astype(jnp.bfloat16),
        preferred_element_type=jnp.float32,
    ) * (1.0 / math.sqrt(HD))
    q_low = q_rot.astype(jnp.bfloat16)

    load_k.wait()
    load_v.wait()
    pl.semaphore_wait(barrier, INST - 1 + HEADS - 1)

    def move(o):
        to = lax.rem(me + o, INST)
        return (
            remote(sk.at[o], rk_ref.at[me], k_send.at[o], k_recv.at[me], to, head),
            remote(sv.at[o], rv_ref.at[me], v_send.at[o], v_recv.at[me], to, head),
        )

    def arrived(o):
        src = lax.rem(me + o, INST)
        return (
            remote(sk.at[o], rk_ref.at[src], k_send.at[o], k_recv.at[src], src, head),
            remote(sv.at[o], rv_ref.at[src], v_send.at[o], v_recv.at[src], src, head),
        )

    def send_blocks(o, _):
        to = lax.rem(me + o, INST)
        for k in range(PER):
            b = plan_ref[to * PER + k]
            sk[o, k] = kc[b]
            sv[o, k] = vc[b]
        for copy in move(o):
            copy.start()
        return 0

    lax.fori_loop(1, INST, send_blocks, 0)

    row_max, row_total, acc = attend(plan_ref, q_low, kc, vc, scores, scale)
    lane = lax.broadcasted_iota(jnp.int32, (ROWS, HD), 1)
    part_send[:, :, :HD] = acc.reshape(16, 8, HD)
    part_send[:, :, HD:] = jnp.where(lane < 64, row_max, row_total).reshape(16, 8, HD)

    def part_copy(t):
        c = lax.rem(chip + t, 16)
        return remote(
            part_send.at[c], part_recv.at[me], part_s.at[t], part_r.at[me], 2 * c, head
        )

    def start_part(t, _):
        part_copy(t).start()
        return 0

    lax.fori_loop(1, 16, start_part, 0)

    @pl.when(core == 1)
    def _():
        part_copy(0).start()

    @pl.when(core == 0)
    def _():
        part_recv[me] = part_send[chip]

        def got_part(o, _):
            src = lax.rem(me + o, INST)
            remote(
                part_send.at[0], part_recv.at[src], part_s.at[0], part_r.at[src], src, head
            ).wait_recv()
            return 0

        lax.fori_loop(1, INST, got_part, 0)
        q_group = qf[pl.ds(pl.multiple_of(chip * 8, 8), 8)].astype(jnp.bfloat16)
        attended = finish_rows(
            part_recv[...],
            chip,
            q_group,
            nk_ref[...],
            nv_ref[...].astype(jnp.float32),
            sign_row,
            rotate,
            scale,
        )
        att[chip] = attended.astype(jnp.bfloat16).astype(jnp.float32)

        def send_att(o, _):
            remote(
                att.at[chip],
                att.at[chip],
                att_s.at[o],
                att_r.at[chip],
                lax.rem(me + o, INST),
                head,
            ).start()
            return 0

        lax.fori_loop(1, INST, send_att, 0)

    def att_from(c):
        return remote(att.at[c], att.at[c], att_s.at[0], att_r.at[c], 2 * c, head)

    def got_att(t, _):
        att_from(lax.rem(chip + t, 16)).wait_recv()
        return 0

    lax.fori_loop(1, 16, got_att, 0)

    @pl.when(core == 1)
    def _():
        att_from(chip).wait_recv()

    everyone = att[...]
    terms = jnp.zeros((16, 256), jnp.float32)
    for h in range(8):
        terms = terms + jnp.dot(
            everyone[:, h, :].astype(jnp.bfloat16),
            w_ref[h * HD : (h + 1) * HD, :],
            preferred_element_type=jnp.float32,
        )
    proj[head] = terms

    def proj_copy(o):
        return remote(
            proj.at[head],
            proj.at[head],
            proj_s.at[o],
            proj_r.at[head],
            me,
            lax.rem(head + o, HEADS),
        )

    def start_proj(o, _):
        proj_copy(o).start()
        return 0

    def got_proj(o, _):
        z = lax.rem(head + o, HEADS)
        remote(proj.at[z], proj.at[z], proj_s.at[o], proj_r.at[z], me, z).wait_recv()
        return 0

    lax.fori_loop(1, HEADS, start_proj, 0)
    lax.fori_loop(1, HEADS, got_proj, 0)
    out_ref[...] = jnp.sum(proj[...], axis=0)

    def sent_proj(o, _):
        proj_copy(o).wait_send()
        return 0

    def sent_part(t, _):
        part_copy(t).wait_send()
        return 0

    lax.fori_loop(1, HEADS, sent_proj, 0)
    lax.fori_loop(1, 16, sent_part, 0)

    @pl.when(core == 1)
    def _():
        part_copy(0).wait_send()

    @pl.when(core == 0)
    def _():
        def sent_att(o, _):
            remote(
                att.at[chip],
                att.at[chip],
                att_s.at[o],
                att_r.at[chip],
                lax.rem(me + o, INST),
                head,
            ).wait_send()
            return 0

        lax.fori_loop(1, INST, sent_att, 0)

    def moved(o, _):
        for copy in move(o):
            copy.wait_send()
        for copy in arrived(o):
            copy.wait_recv()
        return 0

    lax.fori_loop(1, INST, moved, 0)


def place_kernel(table_ref, proj_ref, rk_ref, rv_ref, out_ref, mk_ref, mv_ref, zeros, sems):
    zeros[...] = jnp.zeros_like(zeros)

    def place(s, _):
        row = table_ref[s]

        @pl.when(row >= 0)
        def _():
            pltpu.make_async_copy(rk_ref.at[row], mk_ref.at[s], sems.at[0]).start()
            pltpu.make_async_copy(rv_ref.at[row], mv_ref.at[s], sems.at[1]).start()

        @pl.when(row < 0)
        def _():
            pltpu.make_async_copy(zeros, mk_ref.at[s], sems.at[0]).start()
            pltpu.make_async_copy(zeros, mv_ref.at[s], sems.at[1]).start()

        return 0

    lax.fori_loop(0, SLOTS, place, 0)
    out_ref[...] = proj_ref[...].astype(jnp.bfloat16)
    pltpu.make_async_copy(rk_ref.at[pl.ds(0, SLOTS)], mk_ref, sems.at[0]).wait()
    pltpu.make_async_copy(rv_ref.at[pl.ds(0, SLOTS)], mv_ref, sems.at[1]).wait()


def move_tables(own, block_req, block_fill, dest_inst, new_slot):
    peers = jnp.arange(INST, dtype=jnp.int32)
    slots = jnp.arange(SLOTS, dtype=jnp.int32)
    ranks = jnp.arange(PER, dtype=jnp.int32)
    dest = dest_inst.reshape(INST, SLOTS)
    own_dest = lax.dynamic_index_in_dim(dest, own, 0, keepdims=False)
    same = (own_dest[:, None] == own_dest[None, :]) & (slots[None, :] < slots[:, None])
    own_rank = jnp.sum(same.astype(jnp.int32), axis=1)
    send = (
        (own_dest[None, None, :] == peers[:, None, None])
        & (own_rank[None, None, :] == ranks[None, :, None])
        & (own_dest[None, None, :] != own)
    )
    send_index = jnp.sum(jnp.where(send, slots[None, None, :], 0), axis=2).reshape(-1)
    to_me = (dest == own) & (peers[:, None] != own)
    rank = jnp.cumsum(to_me.astype(jnp.int32), axis=1) - 1
    row = jnp.where(to_me, peers[:, None] * PER + rank, -1).reshape(-1)
    lands = to_me.reshape(-1)[None, :] & (new_slot[None, :] == slots[:, None])
    table = jnp.max(jnp.where(lands, row[None, :], -1), axis=1)
    own_req = lax.dynamic_index_in_dim(block_req.reshape(INST, SLOTS), own, 0, keepdims=False)
    own_fill = lax.dynamic_index_in_dim(block_fill.reshape(INST, SLOTS), own, 0, keepdims=False)
    return jnp.concatenate([send_index, own_req, own_fill]), table


def shards(
    query,
    new_keys,
    new_values,
    cache_keys,
    cache_values,
    signs,
    block_req,
    block_fill,
    dest_inst,
    new_slot,
    out_weight,
):
    own = lax.axis_index("inst")
    plan, table = move_tables(own, block_req, block_fill, dest_inst, new_slot)
    vmem = pl.BlockSpec(memory_space=pltpu.VMEM)
    smem = pl.BlockSpec(memory_space=pltpu.SMEM)
    hbm = pl.BlockSpec(memory_space=pl.ANY)
    blocks = jax.ShapeDtypeStruct((INST, PER, BT, HD), jnp.bfloat16)
    dma = pltpu.SemaphoreType.DMA
    proj, got_keys, got_values = pl.pallas_call(
        layer_kernel,
        out_shape=(jax.ShapeDtypeStruct((16, 256), jnp.float32), blocks, blocks),
        in_specs=[smem, vmem, vmem, vmem, vmem, vmem, hbm, hbm],
        out_specs=(vmem, hbm, hbm),
        scratch_shapes=[
            pltpu.VMEM((SLOTS, BT, HD), jnp.bfloat16),
            pltpu.VMEM((SLOTS, BT, HD), jnp.bfloat16),
            pltpu.VMEM((INST, PER, BT, HD), jnp.bfloat16),
            pltpu.VMEM((INST, PER, BT, HD), jnp.bfloat16),
            pltpu.VMEM((SLOTS // CHUNK, ROWS, CHUNK * BT), jnp.float32),
            pltpu.VMEM((ROWS, HD), jnp.float32),
            pltpu.VMEM((16, 8, 2 * HD), jnp.float32),
            pltpu.VMEM((INST, 8, 2 * HD), jnp.float32),
            pltpu.VMEM((16, 8, HD), jnp.float32),
            pltpu.VMEM((HEADS, 16, 256), jnp.float32),
            dma((2,)),
            dma((INST,)),
            dma((INST,)),
            dma((INST,)),
            dma((INST,)),
            dma((16,)),
            dma((INST,)),
            dma((INST,)),
            dma((16,)),
            dma((HEADS,)),
            dma((HEADS,)),
        ],
        compiler_params=pltpu.CompilerParams(
            collective_id=0, has_side_effects=True, vmem_limit_bytes=48 * 2**20
        ),
    )(
        plan,
        query.reshape(ROWS, HD),
        new_keys.reshape(16, HD),
        new_values.reshape(16, HD),
        signs,
        out_weight,
        cache_keys.reshape(SLOTS, BT, HD),
        cache_values.reshape(SLOTS, BT, HD),
    )
    layer_out, moved_keys, moved_values = pl.pallas_call(
        place_kernel,
        out_shape=(
            jax.ShapeDtypeStruct((16, 256), jnp.bfloat16),
            jax.ShapeDtypeStruct((SLOTS, BT, HD), jnp.bfloat16),
            jax.ShapeDtypeStruct((SLOTS, BT, HD), jnp.bfloat16),
        ),
        in_specs=[smem, vmem, hbm, hbm],
        out_specs=(vmem, hbm, hbm),
        scratch_shapes=[pltpu.VMEM((BT, HD), jnp.bfloat16), dma((2,))],
    )(
        table,
        proj,
        got_keys.reshape(INST * PER, BT, HD),
        got_values.reshape(INST * PER, BT, HD),
    )
    return (
        layer_out.reshape(2, 8, 256),
        moved_keys.reshape(SLOTS, BT, 1, HD),
        moved_values.reshape(SLOTS, BT, 1, HD),
    )


def solution(mesh):
    placed = (
        P(None, None, "head", None),
        P(None, None, "head", None),
        P(None, None, "head", None),
        P("inst", None, "head", None),
        P("inst", None, "head", None),
        P("head", None),
        P(),
        P(),
        P(),
        P(),
        P("head", "inst"),
    )
    return jax.shard_map(
        shards,
        mesh=mesh,
        in_specs=placed,
        out_specs=(
            P(None, None, "inst"),
            P("inst", None, "head", None),
            P("inst", None, "head", None),
        ),
        check_vma=False,
    )
```

```python
import functools
import math

import jax
import jax.numpy as jnp
import numpy as np
from jax import lax
from jax.experimental import pallas as pl
from jax.experimental.pallas import tpu as pltpu
from jax.sharding import PartitionSpec as P

NEG_FILL = -1e30
HIGHEST = lax.Precision.HIGHEST
MESH = pl.DeviceIdType.MESH
INST = 32
HEADS = 8
PER = 4
SLOTS = 64
BT = 128
HD = 128
ROWS = 128
CHUNK = 4
GROUP = 8
SPLITS = (((0, 1), (2, 3)), ((0, 2), (1, 3)), ((0, 3), (1, 2)))
VARIANTS = ((0, 6, 6), (0, 8, 8))
T_U, T_V, SRC_K, DST_K, SRC_V, DST_V, REQ, FILL, PLAN = 0, 128, 256, 264, 272, 280, 288, 352, 416


def hadamard(order_size):
    common = jnp.bitwise_and(
        lax.broadcasted_iota(jnp.int32, (order_size, order_size), 0),
        lax.broadcasted_iota(jnp.int32, (order_size, order_size), 1),
    )
    parity = common
    for shift in (4, 2, 1):
        parity = jnp.bitwise_xor(parity, jnp.right_shift(parity, shift))
    return (1 - 2 * jnp.bitwise_and(parity, 1)).astype(jnp.float32)


def remote(src, dst, send_sem, recv_sem, inst, head):
    return pltpu.make_async_remote_copy(
        src_ref=src,
        dst_ref=dst,
        send_sem=send_sem,
        recv_sem=recv_sem,
        device_id=(inst, head),
        device_id_type=MESH,
    )


def attend(plan_ref, q_low, kc, vc, scores, scale):
    row_req = lax.broadcasted_iota(jnp.int32, (ROWS, BT), 0) // 8 % 8
    token = lax.broadcasted_iota(jnp.int32, (ROWS, BT), 1)
    chunks = SLOTS // CHUNK

    def score_chunk(i, top):
        keys = kc[pl.ds(i * CHUNK, CHUNK)].reshape(CHUNK * BT, HD)
        s = lax.dot_general(
            q_low, keys, (((1,), (1,)), ((), ())), preferred_element_type=jnp.float32
        )
        for c in range(CHUNK):
            req = plan_ref[REQ + i * CHUNK + c]
            fill = plan_ref[FILL + i * CHUNK + c]
            live = (row_req == req) & (token < fill)
            part = jnp.where(live, s[:, c * BT : (c + 1) * BT] * scale, NEG_FILL)
            scores[i, :, c * BT : (c + 1) * BT] = part
            top = jnp.maximum(top, part)
        return top

    top = lax.fori_loop(0, chunks, score_chunk, jnp.full((ROWS, BT), NEG_FILL, jnp.float32))
    row_max = jnp.max(top, axis=1, keepdims=True)

    def value_chunk(i, carry):
        total, acc = carry
        p = jnp.exp(scores[i] - row_max)
        for c in range(CHUNK):
            total = total + p[:, c * BT : (c + 1) * BT]
        values = vc[pl.ds(i * CHUNK, CHUNK)].reshape(CHUNK * BT, HD)
        acc = acc + jnp.dot(p.astype(jnp.bfloat16), values, preferred_element_type=jnp.float32)
        return total, acc

    zero = jnp.zeros((ROWS, BT), jnp.float32)
    total, acc = lax.fori_loop(0, chunks, value_chunk, (zero, zero))
    return row_max, jnp.sum(total, axis=1, keepdims=True), acc


def finish_rows(parts, group, q_group, nk, nv, sign_row, rotate, scale):
    req, step = group % 8, group // 8
    part_max = parts[:, :, HD : HD + 1]
    part_total = parts[:, :, HD + 64 : HD + 65]
    cache_max = jnp.max(part_max, axis=0)
    factor = jnp.exp(part_max - cache_max[None])
    cache_total = jnp.sum(part_total * factor, axis=0)
    cache_sum = jnp.sum(parts[:, :, :HD] * factor, axis=0)
    new_scores = (
        lax.dot_general(q_group, nk, (((1,), (1,)), ((), ())), preferred_element_type=jnp.float32)
        * scale
    )
    col = lax.broadcasted_iota(jnp.int32, (8, 16), 1)
    causal = (col % 8 == req) & (col // 8 <= step)
    new_scores = jnp.where(causal, new_scores, NEG_FILL)
    joined_max = jnp.maximum(cache_max, jnp.max(new_scores, axis=1, keepdims=True))
    cache_factor = jnp.exp(cache_max - joined_max)
    weights = jnp.where(causal, jnp.exp(new_scores - joined_max), 0.0)
    denominator = cache_factor * cache_total + jnp.sum(weights, axis=1, keepdims=True)
    back = jnp.dot(
        cache_factor * cache_sum, rotate, precision=HIGHEST, preferred_element_type=jnp.float32
    )
    back = back * sign_row * (1.0 / math.sqrt(HD))
    fresh = jnp.dot(weights, nv, precision=HIGHEST, preferred_element_type=jnp.float32)
    return (back + fresh) / denominator


def coordinates(inst, split):
    x, y = inst // 8, inst // 2 % 4
    code = jnp.bitwise_xor(x, x // 2) + 4 * jnp.bitwise_xor(y, y // 2)
    (a0, a1), (b0, b1) = SPLITS[split]

    def bit(b):
        return code // (1 << b) % 2

    return bit(a0) + 2 * bit(a1), bit(b0) + 2 * bit(b1), inst % 2


def instance(u, v, core, split):
    (a0, a1), (b0, b1) = SPLITS[split]
    code = (u % 2) * (1 << a0) + (u // 2) * (1 << a1) + (v % 2) * (1 << b0) + (v // 2) * (1 << b1)
    gx, gy = code % 4, code // 4
    return jnp.bitwise_xor(gx, gx // 2) * 8 + jnp.bitwise_xor(gy, gy // 2) * 2 + core


def layer_kernel(split, cap1, cap2, *refs):
    (
        plan_ref,
        q_ref,
        nk_ref,
        nv_ref,
        signs_ref,
        w_ref,
        ck_ref,
        cv_ref,
        out_ref,
        rk_ref,
        rv_ref,
        kc,
        vc,
        first_send,
        mid_k0,
        mid_k1,
        mid_v0,
        mid_v1,
        second_send,
        scores,
        qf,
        part_send,
        part_recv,
        att,
        proj,
        load_sem,
        first_s,
        first_r,
        second_s,
        second_r,
        part_s,
        part_r,
        att_s,
        att_r,
        proj_s,
        proj_r,
    ) = refs
    me = lax.axis_index("inst")
    head = lax.axis_index("head")
    chip, core = me // 2, me % 2
    u, v, _ = coordinates(me, split)
    scale = 1.0 / math.sqrt(HD)
    caches = (kc, vc)
    mids = ((mid_k0, mid_k1), (mid_v0, mid_v1))
    lands = (rk_ref, rv_ref)
    tables = (T_U, T_V)
    sources = (SRC_K, SRC_V)
    dests = (DST_K, DST_V)

    load_k = pltpu.make_async_copy(ck_ref, kc, load_sem.at[0])
    load_v = pltpu.make_async_copy(cv_ref, vc, load_sem.at[1])
    load_k.start()
    load_v.start()

    barrier = pltpu.get_barrier_semaphore()

    def greet_inst(o, _):
        pl.semaphore_signal(
            barrier, inc=1, device_id=(lax.rem(me + o, INST), head), device_id_type=MESH
        )
        return 0

    def greet_head(o, _):
        pl.semaphore_signal(
            barrier, inc=1, device_id=(me, lax.rem(head + o, HEADS)), device_id_type=MESH
        )
        return 0

    lax.fori_loop(1, INST, greet_inst, 0)
    lax.fori_loop(1, HEADS, greet_head, 0)

    sign_row = (2 * signs_ref[...] - 1).astype(jnp.float32)
    rotate = hadamard(HD)
    raw = q_ref[...].astype(jnp.float32)
    qf[...] = raw
    q_rot = jnp.dot(
        (raw * sign_row).astype(jnp.bfloat16),
        rotate.astype(jnp.bfloat16),
        preferred_element_type=jnp.float32,
    ) * (1.0 / math.sqrt(HD))
    q_low = q_rot.astype(jnp.bfloat16)

    load_k.wait()
    load_v.wait()
    pl.semaphore_wait(barrier, INST - 1 + HEADS - 1)

    def peer(plane, along_first, d, j):
        if (plane == 0) == along_first:
            return instance(jnp.bitwise_xor(u, d), v, j, split)
        return instance(u, jnp.bitwise_xor(v, d), j, split)

    def first_copy(plane, half, d, j):
        src = first_send.at[plane, half, d * 2 + j]
        dst = mids[plane][half].at[pl.ds((d * 2 + core) * GROUP, cap1)]
        sems = first_s.at[plane, half, d * 2 + j], first_r.at[plane, half, d * 2 + core]
        return remote(src, dst, *sems, peer(plane, True, d, j), head)

    def first_keep(plane, half):
        return pltpu.make_async_copy(
            first_send.at[plane, half, core],
            mids[plane][half].at[pl.ds(core * GROUP, cap1)],
            first_r.at[plane, half, core],
        )

    def first_wait(plane, half, d, j):
        dst = mids[plane][half].at[pl.ds((d * 2 + j) * GROUP, cap1)]
        return pltpu.make_async_copy(dst, dst, first_r.at[plane, half, d * 2 + j])

    def second_copy(plane, half, d, j):
        src = second_send.at[plane, half, d * 2 + j]
        dst = lands[plane].at[pl.ds((half * 8 + d * 2 + core) * GROUP, cap2)]
        sems = second_s.at[plane, half, d * 2 + j], second_r.at[plane, half, d * 2 + core]
        return remote(src, dst, *sems, peer(plane, False, d, j), head)

    def second_keep(plane, half):
        return pltpu.make_async_copy(
            second_send.at[plane, half, core],
            lands[plane].at[pl.ds((half * 8 + core) * GROUP, cap2)],
            second_r.at[plane, half, core],
        )

    def second_wait(plane, half, d, j):
        dst = lands[plane].at[pl.ds((half * 8 + d * 2 + j) * GROUP, cap2)]
        return pltpu.make_async_copy(dst, dst, second_r.at[plane, half, d * 2 + j])

    def start_first(half):
        def body(t, _):
            d, j = 3 - t // 2, t % 2
            for plane in range(2):
                first = jnp.bitwise_xor(u if plane == 0 else v, d)
                for m in range(cap1):
                    b = plan_ref[tables[plane] + first * 32 + m * PER + j * 2 + half]
                    first_send[plane, half, d * 2 + j, m] = caches[plane][b]

                @pl.when((d > 0) | (j != core))
                def _(plane=plane):
                    first_copy(plane, half, d, j).start()

                @pl.when((d == 0) & (j == core))
                def _(plane=plane):
                    first_keep(plane, half).start()

            return 0

        lax.fori_loop(0, 8, body, 0)

    def start_second(half):
        def wait_body(t, _):
            for plane in range(2):
                first_wait(plane, half, t // 2, t % 2).wait()
            return 0

        lax.fori_loop(0, 8, wait_body, 0)

        def body(t, _):
            d, j = 3 - t // 2, t % 2
            for plane in range(2):
                base = plan_ref[dests[plane] + d * 2 + j]
                for n in range(cap2):
                    b = base + plan_ref[sources[plane] + n]
                    second_send[plane, half, d * 2 + j, n] = mids[plane][half][b]

                @pl.when((d > 0) | (j != core))
                def _(plane=plane):
                    second_copy(plane, half, d, j).start()

                @pl.when((d == 0) & (j == core))
                def _(plane=plane):
                    second_keep(plane, half).start()

            return 0

        lax.fori_loop(0, 8, body, 0)

    start_first(0)
    start_first(1)

    row_max, row_total, acc = attend(plan_ref, q_low, kc, vc, scores, scale)
    lane = lax.broadcasted_iota(jnp.int32, (ROWS, HD), 1)
    part_send[:, :, :HD] = acc.reshape(16, 8, HD)
    part_send[:, :, HD:] = jnp.where(lane < 64, row_max, row_total).reshape(16, 8, HD)

    def part_copy(t):
        c = lax.rem(chip + t, 16)
        return remote(
            part_send.at[c], part_recv.at[me], part_s.at[t], part_r.at[me], 2 * c, head
        )

    def start_part(t, _):
        part_copy(t).start()
        return 0

    lax.fori_loop(1, 16, start_part, 0)

    @pl.when(core == 1)
    def _():
        part_copy(0).start()

    start_second(0)

    @pl.when(core == 0)
    def _():
        part_recv[me] = part_send[chip]

        def got_part(o, _):
            src = lax.rem(me + o, INST)
            remote(
                part_send.at[0], part_recv.at[src], part_s.at[0], part_r.at[src], src, head
            ).wait_recv()
            return 0

        lax.fori_loop(1, INST, got_part, 0)
        q_group = qf[pl.ds(pl.multiple_of(chip * 8, 8), 8)].astype(jnp.bfloat16)
        attended = finish_rows(
            part_recv[...],
            chip,
            q_group,
            nk_ref[...],
            nv_ref[...].astype(jnp.float32),
            sign_row,
            rotate,
            scale,
        )
        att[chip] = attended.astype(jnp.bfloat16).astype(jnp.float32)

        def send_att(o, _):
            remote(
                att.at[chip],
                att.at[chip],
                att_s.at[o],
                att_r.at[chip],
                lax.rem(me + o, INST),
                head,
            ).start()
            return 0

        lax.fori_loop(1, INST, send_att, 0)

    start_second(1)

    def att_from(c):
        return remote(att.at[c], att.at[c], att_s.at[0], att_r.at[c], 2 * c, head)

    def got_att(t, _):
        att_from(lax.rem(chip + t, 16)).wait_recv()
        return 0

    lax.fori_loop(1, 16, got_att, 0)

    @pl.when(core == 1)
    def _():
        att_from(chip).wait_recv()

    everyone = att[...]
    terms = jnp.zeros((16, 256), jnp.float32)
    for h in range(8):
        terms = terms + jnp.dot(
            everyone[:, h, :].astype(jnp.bfloat16),
            w_ref[h * HD : (h + 1) * HD, :],
            preferred_element_type=jnp.float32,
        )
    proj[head] = terms

    def proj_copy(o):
        return remote(
            proj.at[head],
            proj.at[head],
            proj_s.at[o],
            proj_r.at[head],
            me,
            lax.rem(head + o, HEADS),
        )

    def start_proj(o, _):
        proj_copy(o).start()
        return 0

    def got_proj(o, _):
        z = lax.rem(head + o, HEADS)
        remote(proj.at[z], proj.at[z], proj_s.at[o], proj_r.at[z], me, z).wait_recv()
        return 0

    lax.fori_loop(1, HEADS, start_proj, 0)
    lax.fori_loop(1, HEADS, got_proj, 0)
    out_ref[...] = jnp.sum(proj[...], axis=0)

    def sent_proj(o, _):
        proj_copy(o).wait_send()
        return 0

    def sent_part(t, _):
        part_copy(t).wait_send()
        return 0

    lax.fori_loop(1, HEADS, sent_proj, 0)
    lax.fori_loop(1, 16, sent_part, 0)

    @pl.when(core == 1)
    def _():
        part_copy(0).wait_send()

    @pl.when(core == 0)
    def _():
        def sent_att(o, _):
            remote(
                att.at[chip],
                att.at[chip],
                att_s.at[o],
                att_r.at[chip],
                lax.rem(me + o, INST),
                head,
            ).wait_send()
            return 0

        lax.fori_loop(1, INST, sent_att, 0)

    def finish(t, _):
        d, j = t // 2, t % 2
        for half in range(2):
            for plane in range(2):

                @pl.when((d > 0) | (j != core))
                def _(plane=plane, half=half):
                    first_copy(plane, half, d, j).wait_send()
                    second_copy(plane, half, d, j).wait_send()

                second_wait(plane, half, d, j).wait()
        return 0

    lax.fori_loop(0, 8, finish, 0)


def layer_call(variant, operands):
    split, cap1, cap2 = VARIANTS[variant]
    vmem = pl.BlockSpec(memory_space=pltpu.VMEM)
    smem = pl.BlockSpec(memory_space=pltpu.SMEM)
    hbm = pl.BlockSpec(memory_space=pl.ANY)
    blocks = jax.ShapeDtypeStruct((2 * 8 * GROUP, BT, HD), jnp.bfloat16)
    dma = pltpu.SemaphoreType.DMA

    def low(*lead):
        return pltpu.VMEM((*lead, BT, HD), jnp.bfloat16)

    return pl.pallas_call(
        functools.partial(layer_kernel, split, cap1, cap2),
        out_shape=(jax.ShapeDtypeStruct((16, 256), jnp.float32), blocks, blocks),
        in_specs=[smem, vmem, vmem, vmem, vmem, vmem, hbm, hbm],
        out_specs=(vmem, hbm, hbm),
        scratch_shapes=[
            low(SLOTS),
            low(SLOTS),
            low(2, 2, 8, cap1),
            low(8 * GROUP),
            low(8 * GROUP),
            low(8 * GROUP),
            low(8 * GROUP),
            low(2, 2, 8, cap2),
            pltpu.VMEM((SLOTS // CHUNK, ROWS, CHUNK * BT), jnp.float32),
            pltpu.VMEM((ROWS, HD), jnp.float32),
            pltpu.VMEM((16, 8, 2 * HD), jnp.float32),
            pltpu.VMEM((INST, 8, 2 * HD), jnp.float32),
            pltpu.VMEM((16, 8, HD), jnp.float32),
            pltpu.VMEM((HEADS, 16, 256), jnp.float32),
            dma((2,)),
            dma((2, 2, 8)),
            dma((2, 2, 8)),
            dma((2, 2, 8)),
            dma((2, 2, 8)),
            dma((16,)),
            dma((INST,)),
            dma((INST,)),
            dma((16,)),
            dma((HEADS,)),
            dma((HEADS,)),
        ],
        compiler_params=pltpu.CompilerParams(
            collective_id=variant, has_side_effects=True, vmem_limit_bytes=56 * 2**20
        ),
    )(*operands)


def place_kernel(table_ref, proj_ref, rk_ref, rv_ref, out_ref, mk_ref, mv_ref, sems):
    lands = ((rk_ref, mk_ref), (rv_ref, mv_ref))

    def place(s, _):
        for plane, (src, dst) in enumerate(lands):
            row = table_ref[plane * SLOTS + s]

            @pl.when(row >= 0)
            def _(plane=plane, src=src, dst=dst, row=row):
                pltpu.make_async_copy(src.at[row], dst.at[s], sems.at[plane]).start()

            @pl.when(row < 0)
            def _(dst=dst):
                dst[s] = jnp.zeros((BT, HD), jnp.bfloat16)

        return 0

    lax.fori_loop(0, SLOTS, place, 0)
    out_ref[...] = proj_ref[...].astype(jnp.bfloat16)

    def settle(s, _):
        for plane, (src, dst) in enumerate(lands):
            row = table_ref[plane * SLOTS + s]

            @pl.when(row >= 0)
            def _(plane=plane, src=src, dst=dst, row=row):
                pltpu.make_async_copy(src.at[row], dst.at[s], sems.at[plane]).wait()

        return 0

    lax.fori_loop(0, SLOTS, settle, 0)


def static_groups():
    out = []
    for (a0, a1), (b0, b1) in SPLITS:
        rows = []
        for inst in range(INST):
            x, y = inst // 8, inst // 2 % 4
            code = (x ^ (x // 2)) + 4 * (y ^ (y // 2))
            bits = [code >> b & 1 for b in range(4)]
            rows.append((bits[a0] + 2 * bits[a1], bits[b0] + 2 * bits[b1]))
        out.append(np.array(rows, np.int32).T)
    return np.stack(out)


def move_plan(own, block_req, block_fill, dest_inst, new_slot):
    i32 = jnp.int32
    peers = jnp.arange(INST, dtype=i32)
    slots = jnp.arange(SLOTS, dtype=i32)
    dest = dest_inst.reshape(INST, SLOTS)
    slot_of = new_slot.reshape(INST, SLOTS)
    released = dest[:, 0] != peers
    groups = static_groups()

    def needs(split):
        u, v = jnp.asarray(groups[split])
        most_kept, most_gone = jnp.zeros((), i32), jnp.zeros((), i32)
        for coord in (u, v):
            inside = coord[None, :] == jnp.arange(4, dtype=i32)[:, None]
            gone = jnp.sum((inside & released[None, :]).astype(i32), axis=1)
            most_gone = jnp.maximum(most_gone, jnp.max(gone))
            most_kept = jnp.maximum(most_kept, 8 - jnp.min(gone))
        return most_kept, most_gone

    need = {split: needs(split) for split in sorted({variant[0] for variant in VARIANTS})}
    choice = jnp.full((), len(VARIANTS) - 1, i32)
    for index in reversed(range(len(VARIANTS) - 1)):
        split, cap1, cap2 = VARIANTS[index]
        fits = (need[split][0] <= cap1) & (need[split][1] <= cap2)
        choice = jnp.where(fits, index, choice)
    used = [split for split, _, _ in VARIANTS]
    coords = jnp.asarray(groups[used[-1]])
    for index in range(len(VARIANTS) - 1):
        if used[index] != used[-1]:
            coords = jnp.where(choice == index, jnp.asarray(groups[used[index]]), coords)
    core = peers % 2
    mine = (peers == own).astype(i32)
    before = peers[None, :] < peers[:, None]
    own_dest = jnp.sum(dest * mine[:, None], axis=0)
    own_rank = jnp.sum(
        ((own_dest[:, None] == own_dest[None, :]) & (slots[None, :] < slots[:, None])).astype(i32),
        axis=1,
    )
    to_me = (dest == own) & released[:, None]
    rank = jnp.sum(
        (to_me[:, None, :] & (slots[None, None, :] < slots[None, :, None])).astype(i32), axis=2
    )
    sends, extras, rows = [], [], []
    for plane in range(2):
        first, second = (coords[0], coords[1]) if plane == 0 else (coords[1], coords[0])
        own_first, own_second = jnp.sum(first * mine), jnp.sum(second * mine)
        kept_rank = jnp.sum(
            ((first[:, None] == first[None, :]) & before & ~released[None, :]).astype(i32), axis=1
        )
        gone_rank = jnp.sum(
            ((second[:, None] == second[None, :]) & before & released[None, :]).astype(i32), axis=1
        )
        place = first * 32 + kept_rank * PER
        sent = jnp.sum(
            jnp.where(own_dest[:, None] == peers[None, :], place[None, :], 0), axis=1
        )
        at = sent + own_rank
        hit = at[None, :] == jnp.arange(128, dtype=i32)[:, None]
        sends.append(jnp.sum(jnp.where(hit, slots[None, :], 0), axis=1))
        lane = jnp.arange(8, dtype=i32)[:, None]
        source = (jnp.bitwise_xor(first, own_first) * 2 + core) * GROUP
        take = released & (second == own_second)
        extras.append(
            jnp.sum(jnp.where(take[None, :] & (gone_rank[None, :] == lane), source[None, :], 0), 1)
        )
        distance = jnp.bitwise_xor(second, own_second) * 2 + core
        take = first == own_first
        extras.append(
            jnp.sum(jnp.where(take[None, :] & (distance[None, :] == lane), kept_rank[None, :], 0), 1)
        )
        base = jnp.bitwise_xor(second, own_second) * 2 * GROUP + gone_rank
        rows.append(
            base[:, None] + (rank // 2) * GROUP + (rank % 2) * 8 * GROUP
        )
    lands = to_me[None] & (slot_of[None] == slots[:, None, None])
    table = [
        jnp.max(jnp.where(lands, row[None], -1), axis=(1, 2)) for row in rows
    ]
    own_req = jnp.sum(block_req.reshape(INST, SLOTS) * mine[:, None], axis=0)
    own_fill = jnp.sum(block_fill.reshape(INST, SLOTS) * mine[:, None], axis=0)
    return choice, jnp.concatenate([*sends, *extras, own_req, own_fill]), jnp.concatenate(table)


def shards(
    query,
    new_keys,
    new_values,
    cache_keys,
    cache_values,
    signs,
    block_req,
    block_fill,
    dest_inst,
    new_slot,
    out_weight,
):
    own = lax.axis_index("inst")
    choice, plan, table = move_plan(own, block_req, block_fill, dest_inst, new_slot)
    operands = (
        plan,
        query.reshape(ROWS, HD),
        new_keys.reshape(16, HD),
        new_values.reshape(16, HD),
        signs,
        out_weight,
        cache_keys.reshape(SLOTS, BT, HD),
        cache_values.reshape(SLOTS, BT, HD),
    )
    branches = [functools.partial(layer_call, variant) for variant in range(len(VARIANTS))]
    proj, got_keys, got_values = lax.switch(choice, branches, operands)
    vmem = pl.BlockSpec(memory_space=pltpu.VMEM)
    smem = pl.BlockSpec(memory_space=pltpu.SMEM)
    hbm = pl.BlockSpec(memory_space=pl.ANY)
    layer_out, moved_keys, moved_values = pl.pallas_call(
        place_kernel,
        out_shape=(
            jax.ShapeDtypeStruct((16, 256), jnp.bfloat16),
            jax.ShapeDtypeStruct((SLOTS, BT, HD), jnp.bfloat16),
            jax.ShapeDtypeStruct((SLOTS, BT, HD), jnp.bfloat16),
        ),
        in_specs=[smem, vmem, hbm, hbm],
        out_specs=(vmem, vmem, vmem),
        scratch_shapes=[pltpu.SemaphoreType.DMA((2,))],
        compiler_params=pltpu.CompilerParams(vmem_limit_bytes=32 * 2**20),
    )(table, proj, got_keys, got_values)
    return (
        layer_out.reshape(2, 8, 256),
        moved_keys.reshape(SLOTS, BT, 1, HD),
        moved_values.reshape(SLOTS, BT, 1, HD),
    )


def solution(mesh):
    placed = (
        P(None, None, "head", None),
        P(None, None, "head", None),
        P(None, None, "head", None),
        P("inst", None, "head", None),
        P("inst", None, "head", None),
        P("head", None),
        P(),
        P(),
        P(),
        P(),
        P("head", "inst"),
    )
    return jax.shard_map(
        shards,
        mesh=mesh,
        in_specs=placed,
        out_specs=(
            P(None, None, "inst"),
            P("inst", None, "head", None),
            P("inst", None, "head", None),
        ),
        check_vma=False,
    )
```

```python
import functools
import math

import jax
import jax.numpy as jnp
import numpy as np
from jax import lax
from jax.experimental import pallas as pl
from jax.experimental.pallas import tpu as pltpu
from jax.sharding import PartitionSpec as P

NEG_FILL = -1e30
HIGHEST = lax.Precision.HIGHEST
MESH = pl.DeviceIdType.MESH
INST = 32
HEADS = 8
PER = 4
SLOTS = 64
BT = 128
HD = 128
ROWS = 128
CHUNK = 4
GROUP = 8
SPLITS = (((0, 1), (2, 3)), ((0, 2), (1, 3)), ((0, 3), (1, 2)))
VARIANTS = (
    (0, 5, 5),
    (1, 5, 5),
    (2, 5, 5),
    (0, 5, 6),
    (1, 5, 6),
    (2, 5, 6),
    (0, 6, 5),
    (1, 6, 5),
    (2, 6, 5),
    (0, 6, 6),
    (1, 6, 6),
    (2, 6, 6),
    (0, 7, 7),
    (0, 8, 8),
)
SEND, SOURCE, DEST, REQ, FILL = 0, 2, 4, 6, 7


def hadamard(order_size):
    common = jnp.bitwise_and(
        lax.broadcasted_iota(jnp.int32, (order_size, order_size), 0),
        lax.broadcasted_iota(jnp.int32, (order_size, order_size), 1),
    )
    parity = common
    for shift in (4, 2, 1):
        parity = jnp.bitwise_xor(parity, jnp.right_shift(parity, shift))
    return (1 - 2 * jnp.bitwise_and(parity, 1)).astype(jnp.float32)


def remote(src, dst, send_sem, recv_sem, inst, head):
    return pltpu.make_async_remote_copy(
        src_ref=src,
        dst_ref=dst,
        send_sem=send_sem,
        recv_sem=recv_sem,
        device_id=(inst, head),
        device_id_type=MESH,
    )


def attend(plan_ref, q_low, kc, vc, scores, scale):
    row_req = lax.broadcasted_iota(jnp.int32, (ROWS, BT), 0) // 8 % 8
    token = lax.broadcasted_iota(jnp.int32, (ROWS, BT), 1)
    chunks = SLOTS // CHUNK

    def score_chunk(i, top):
        keys = kc[pl.ds(i * CHUNK, CHUNK)].reshape(CHUNK * BT, HD)
        s = lax.dot_general(
            q_low, keys, (((1,), (1,)), ((), ())), preferred_element_type=jnp.float32
        )
        for c in range(CHUNK):
            req = plan_ref[REQ, i * CHUNK + c]
            fill = plan_ref[FILL, i * CHUNK + c]
            live = (row_req == req) & (token < fill)
            part = jnp.where(live, s[:, c * BT : (c + 1) * BT] * scale, NEG_FILL)
            scores[i, :, c * BT : (c + 1) * BT] = part
            top = jnp.maximum(top, part)
        return top

    top = lax.fori_loop(0, chunks, score_chunk, jnp.full((ROWS, BT), NEG_FILL, jnp.float32))
    row_max = jnp.max(top, axis=1, keepdims=True)

    def value_chunk(i, carry):
        total, acc = carry
        p = jnp.exp(scores[i] - row_max)
        for c in range(CHUNK):
            total = total + p[:, c * BT : (c + 1) * BT]
        values = vc[pl.ds(i * CHUNK, CHUNK)].reshape(CHUNK * BT, HD)
        acc = acc + jnp.dot(p.astype(jnp.bfloat16), values, preferred_element_type=jnp.float32)
        return total, acc

    zero = jnp.zeros((ROWS, BT), jnp.float32)
    total, acc = lax.fori_loop(0, chunks, value_chunk, (zero, zero))
    return row_max, jnp.sum(total, axis=1, keepdims=True), acc


def finish_rows(parts, group, q_group, nk, nv, sign_row, rotate, scale):
    req, step = group % 8, group // 8
    part_max = parts[:, :, HD : HD + 1]
    part_total = parts[:, :, HD + 64 : HD + 65]
    cache_max = jnp.max(part_max, axis=0)
    factor = jnp.exp(part_max - cache_max[None])
    cache_total = jnp.sum(part_total * factor, axis=0)
    cache_sum = jnp.sum(parts[:, :, :HD] * factor, axis=0)
    new_scores = (
        lax.dot_general(q_group, nk, (((1,), (1,)), ((), ())), preferred_element_type=jnp.float32)
        * scale
    )
    col = lax.broadcasted_iota(jnp.int32, (8, 16), 1)
    causal = (col % 8 == req) & (col // 8 <= step)
    new_scores = jnp.where(causal, new_scores, NEG_FILL)
    joined_max = jnp.maximum(cache_max, jnp.max(new_scores, axis=1, keepdims=True))
    cache_factor = jnp.exp(cache_max - joined_max)
    weights = jnp.where(causal, jnp.exp(new_scores - joined_max), 0.0)
    denominator = cache_factor * cache_total + jnp.sum(weights, axis=1, keepdims=True)
    back = jnp.dot(
        cache_factor * cache_sum, rotate, precision=HIGHEST, preferred_element_type=jnp.float32
    )
    back = back * sign_row * (1.0 / math.sqrt(HD))
    fresh = jnp.dot(weights, nv, precision=HIGHEST, preferred_element_type=jnp.float32)
    return (back + fresh) / denominator


def coordinates(inst, split):
    x, y = inst // 8, inst // 2 % 4
    code = jnp.bitwise_xor(x, x // 2) + 4 * jnp.bitwise_xor(y, y // 2)
    (a0, a1), (b0, b1) = SPLITS[split]

    def bit(b):
        return code // (1 << b) % 2

    return bit(a0) + 2 * bit(a1), bit(b0) + 2 * bit(b1), inst % 2


def instance(u, v, core, split):
    (a0, a1), (b0, b1) = SPLITS[split]
    code = (u % 2) * (1 << a0) + (u // 2) * (1 << a1) + (v % 2) * (1 << b0) + (v // 2) * (1 << b1)
    gx, gy = code % 4, code // 4
    return jnp.bitwise_xor(gx, gx // 2) * 8 + jnp.bitwise_xor(gy, gy // 2) * 2 + core


def lanes_to_rows(row, count):
    sub = lax.broadcasted_iota(jnp.int32, (count, 128), 0)
    lane = lax.broadcasted_iota(jnp.int32, (count, 128), 1)
    return jnp.sum(jnp.where(sub == lane, row, 0), axis=1, keepdims=True)


def moved_elements(dest):
    sub = lax.broadcasted_iota(jnp.int32, (16, 128), 0)
    lane = lax.broadcasted_iota(jnp.int32, (16, 128), 1)
    return (dest != 2 * sub + lane // 64).astype(jnp.int32)


def released_row(dest):
    moved = moved_elements(dest)
    sub = lax.broadcasted_iota(jnp.int32, (16, 128), 0)
    lane = lax.broadcasted_iota(jnp.int32, (16, 128), 1)
    pick = jnp.where(lane % 2 == 0, moved[:, 0:1], moved[:, 64:65])
    return jnp.sum(jnp.where(lane // 2 == sub, pick, 0), axis=0, keepdims=True)


def own_half(ref, me):
    row = ref[pl.ds(me // 2, 1), :]
    return jnp.where(me % 2 == 1, jnp.concatenate([row[:, 64:], row[:, :64]], axis=1), row)


def write_plan(split, me, dest_ref, req_ref, fill_ref, plan):
    dest = dest_ref[...]
    sub = lax.broadcasted_iota(jnp.int32, (32, 128), 0)
    lane = lax.broadcasted_iota(jnp.int32, (32, 128), 1)
    sub_all = lax.broadcasted_iota(jnp.int32, (128, 128), 0)
    lane_all = lax.broadcasted_iota(jnp.int32, (128, 128), 1)
    gone_row = released_row(dest)
    kept_row = jnp.where(lane[:1] < INST, 1 - gone_row, 0)
    gone = lanes_to_rows(gone_row, 32)
    at_row = coordinates(lane, split)
    at_col = coordinates(sub, split)
    at_me = coordinates(me, split)
    own = own_half(dest_ref, me)
    own_col = lanes_to_rows(own, 128)
    rank = jnp.sum(
        ((own_col == own) & (sub_all < lane_all)).astype(jnp.int32), axis=0, keepdims=True
    )
    for plane in range(2):
        one, two = plane, 1 - plane
        kept_rank = jnp.sum(
            jnp.where((at_col[one] == at_row[one]) & (lane < sub), kept_row, 0),
            axis=1,
            keepdims=True,
        )
        gone_rank = jnp.sum(
            jnp.where((at_col[two] == at_row[two]) & (lane < sub), gone_row, 0),
            axis=1,
            keepdims=True,
        )
        place = at_col[one] * 32 + kept_rank * PER
        at = jnp.sum(jnp.where(sub == own, place, 0), axis=0, keepdims=True) + rank
        at = jnp.where(lane[:1] < SLOTS, at, -1)
        hit = lanes_to_rows(at, 128) == lane_all
        plan[SEND + plane : SEND + plane + 1] = jnp.sum(
            jnp.where(hit, sub_all, 0), axis=0, keepdims=True
        )
        source = (jnp.bitwise_xor(at_col[one], at_me[one]) * 2 + at_col[2]) * GROUP
        take = (gone == 1) & (at_col[two] == at_me[two]) & (gone_rank == lane)
        plan[SOURCE + plane : SOURCE + plane + 1] = jnp.sum(
            jnp.where(take, source, 0), axis=0, keepdims=True
        )
        distance = jnp.bitwise_xor(at_col[two], at_me[two]) * 2 + at_col[2]
        take = (at_col[one] == at_me[one]) & (distance == lane)
        plan[DEST + plane : DEST + plane + 1] = jnp.sum(
            jnp.where(take, kept_rank, 0), axis=0, keepdims=True
        )
    plan[REQ : REQ + 1] = own_half(req_ref, me)
    plan[FILL : FILL + 1] = own_half(fill_ref, me)


def arrival_table(split, me, dest, slot):
    sub = lax.broadcasted_iota(jnp.int32, (16, 128), 0)
    lane = lax.broadcasted_iota(jnp.int32, (16, 128), 1)
    source = 2 * sub + lane // 64
    to_me = (dest == me) & (moved_elements(dest) == 1)
    count = to_me.astype(jnp.int32)
    for step in (1, 2, 4, 8, 16, 32):
        shifted = jnp.concatenate([count[:, 128 - step :], count[:, : 128 - step]], axis=1)
        count = count + jnp.where(lane % 64 >= step, shifted, 0)
    rank = count - 1
    gone_row = released_row(dest)
    at_row = coordinates(lane, split)
    at_me = coordinates(me, split)
    landed = jnp.zeros((16, 128), jnp.int32)
    for plane in range(2):
        two = 1 - plane
        ranks = []
        for core in range(2):
            inst = 2 * sub + core
            same = (coordinates(inst, split)[two] == at_row[two]) & (lane < inst)
            ranks.append(jnp.sum(jnp.where(same, gone_row, 0), axis=1, keepdims=True))
        gone_rank = jnp.where(lane < 64, ranks[0], ranks[1])
        far = jnp.bitwise_xor(coordinates(source, split)[two], at_me[two])
        row = far * 2 * GROUP + gone_rank + rank // 2 * GROUP + rank % 2 * 8 * GROUP
        landed = landed * 128 + row
    landed = jnp.where(to_me, landed, -1)
    want = lax.broadcasted_iota(jnp.int32, (SLOTS, 128), 0)
    found = jnp.full((SLOTS, 128), -1, jnp.int32)
    for i in range(16):
        found = jnp.maximum(
            found, jnp.where(slot[i : i + 1] == want, landed[i : i + 1], -1)
        )
    column = jnp.max(found, axis=1, keepdims=True)
    spread = jnp.where(want == lax.broadcasted_iota(jnp.int32, (SLOTS, 128), 1), column + 1, 0)
    return jnp.broadcast_to(jnp.sum(spread, axis=0, keepdims=True) - 1, (8, 128))


def choose_kernel(dest_ref, choice_ref):
    gone = [(dest_ref[inst * SLOTS] != inst).astype(jnp.int32) for inst in range(INST)]
    groups = static_groups()
    need = []
    for split in range(len(SPLITS)):
        counts = []
        for coord in range(2):
            for group in range(4):
                members = [gone[i] for i in range(INST) if groups[split][coord][i] == group]
                counts.append(functools.reduce(jnp.add, members))
        most = functools.reduce(jnp.maximum, counts)
        least = functools.reduce(jnp.minimum, counts)
        need.append((8 - least, most))
    choice = jnp.full((), len(VARIANTS) - 1, jnp.int32)
    for index in reversed(range(len(VARIANTS) - 1)):
        split, cap1, cap2 = VARIANTS[index]
        fits = (need[split][0] <= cap1) & (need[split][1] <= cap2)
        choice = jnp.where(fits, index, choice)
    choice_ref[0] = choice


def layer_kernel(split, cap1, cap2, *refs):
    (
        dest_ref,
        slot_ref,
        req_ref,
        fill_ref,
        q_ref,
        nk_ref,
        nv_ref,
        signs_ref,
        w_ref,
        ck_ref,
        cv_ref,
        out_ref,
        table_ref,
        rk_ref,
        rv_ref,
        plan_vmem,
        plan_ref,
        kc,
        vc,
        first_send,
        mid_k0,
        mid_k1,
        mid_v0,
        mid_v1,
        second_send,
        scores,
        qf,
        part_send,
        part_recv,
        att,
        proj,
        load_sem,
        plan_sem,
        first_s,
        first_r,
        second_s,
        second_r,
        part_s,
        part_r,
        att_s,
        att_r,
        proj_s,
        proj_r,
    ) = refs
    me = lax.axis_index("inst")
    head = lax.axis_index("head")
    chip, core = me // 2, me % 2
    u, v, _ = coordinates(me, split)
    scale = 1.0 / math.sqrt(HD)
    caches = (kc, vc)
    mids = ((mid_k0, mid_k1), (mid_v0, mid_v1))
    lands = (rk_ref, rv_ref)

    load_k = pltpu.make_async_copy(ck_ref, kc, load_sem.at[0])
    load_v = pltpu.make_async_copy(cv_ref, vc, load_sem.at[1])
    load_k.start()
    load_v.start()

    barrier = pltpu.get_barrier_semaphore()

    def greet_inst(o, _):
        pl.semaphore_signal(
            barrier, inc=1, device_id=(lax.rem(me + o, INST), head), device_id_type=MESH
        )
        return 0

    def greet_head(o, _):
        pl.semaphore_signal(
            barrier, inc=1, device_id=(me, lax.rem(head + o, HEADS)), device_id_type=MESH
        )
        return 0

    lax.fori_loop(1, INST, greet_inst, 0)
    lax.fori_loop(1, HEADS, greet_head, 0)

    write_plan(split, me, dest_ref, req_ref, fill_ref, plan_vmem)
    to_smem = pltpu.make_async_copy(plan_vmem, plan_ref, plan_sem)
    to_smem.start()

    sign_row = (2 * signs_ref[...] - 1).astype(jnp.float32)
    rotate = hadamard(HD)
    raw = q_ref[...].astype(jnp.float32)
    qf[...] = raw
    q_rot = jnp.dot(
        (raw * sign_row).astype(jnp.bfloat16),
        rotate.astype(jnp.bfloat16),
        preferred_element_type=jnp.float32,
    ) * (1.0 / math.sqrt(HD))
    q_low = q_rot.astype(jnp.bfloat16)

    to_smem.wait()
    load_k.wait()
    load_v.wait()
    pl.semaphore_wait(barrier, INST - 1 + HEADS - 1)

    def peer(plane, along_first, d, j):
        if (plane == 0) == along_first:
            return instance(jnp.bitwise_xor(u, d), v, j, split)
        return instance(u, jnp.bitwise_xor(v, d), j, split)

    def first_copy(plane, half, d, j):
        src = first_send.at[plane, half, d * 2 + j]
        dst = mids[plane][half].at[pl.ds((d * 2 + core) * GROUP, cap1)]
        sems = first_s.at[plane, half, d * 2 + j], first_r.at[plane, half, d * 2 + core]
        return remote(src, dst, *sems, peer(plane, True, d, j), head)

    def first_keep(plane, half):
        return pltpu.make_async_copy(
            first_send.at[plane, half, core],
            mids[plane][half].at[pl.ds(core * GROUP, cap1)],
            first_r.at[plane, half, core],
        )

    def first_wait(plane, half, d, j):
        dst = mids[plane][half].at[pl.ds((d * 2 + j) * GROUP, cap1)]
        return pltpu.make_async_copy(dst, dst, first_r.at[plane, half, d * 2 + j])

    def second_copy(plane, half, d, j):
        src = second_send.at[plane, half, d * 2 + j]
        dst = lands[plane].at[pl.ds((half * 8 + d * 2 + core) * GROUP, cap2)]
        sems = second_s.at[plane, half, d * 2 + j], second_r.at[plane, half, d * 2 + core]
        return remote(src, dst, *sems, peer(plane, False, d, j), head)

    def second_keep(plane, half):
        return pltpu.make_async_copy(
            second_send.at[plane, half, core],
            lands[plane].at[pl.ds((half * 8 + core) * GROUP, cap2)],
            second_r.at[plane, half, core],
        )

    def second_wait(plane, half, d, j):
        dst = lands[plane].at[pl.ds((half * 8 + d * 2 + j) * GROUP, cap2)]
        return pltpu.make_async_copy(dst, dst, second_r.at[plane, half, d * 2 + j])

    def start_first(half):
        def body(t, _):
            d, j = 3 - t // 2, t % 2
            for plane in range(2):
                first = jnp.bitwise_xor(u if plane == 0 else v, d)
                for m in range(cap1):
                    b = plan_ref[SEND + plane, first * 32 + m * PER + j * 2 + half]
                    first_send[plane, half, d * 2 + j, m] = caches[plane][b]

                @pl.when((d > 0) | (j != core))
                def _(plane=plane):
                    first_copy(plane, half, d, j).start()

                @pl.when((d == 0) & (j == core))
                def _(plane=plane):
                    first_keep(plane, half).start()

            return 0

        lax.fori_loop(0, 8, body, 0)

    def start_second(half):
        def wait_body(t, _):
            for plane in range(2):
                first_wait(plane, half, t // 2, t % 2).wait()
            return 0

        lax.fori_loop(0, 8, wait_body, 0)

        def body(t, _):
            d, j = 3 - t // 2, t % 2
            for plane in range(2):
                base = plan_ref[DEST + plane, d * 2 + j]
                for n in range(cap2):
                    b = base + plan_ref[SOURCE + plane, n]
                    second_send[plane, half, d * 2 + j, n] = mids[plane][half][b]

                @pl.when((d > 0) | (j != core))
                def _(plane=plane):
                    second_copy(plane, half, d, j).start()

                @pl.when((d == 0) & (j == core))
                def _(plane=plane):
                    second_keep(plane, half).start()

            return 0

        lax.fori_loop(0, 8, body, 0)

    start_first(0)
    start_first(1)

    row_max, row_total, acc = attend(plan_ref, q_low, kc, vc, scores, scale)
    lane = lax.broadcasted_iota(jnp.int32, (ROWS, HD), 1)
    part_send[:, :, :HD] = acc.reshape(16, 8, HD)
    part_send[:, :, HD:] = jnp.where(lane < 64, row_max, row_total).reshape(16, 8, HD)

    def part_copy(t):
        c = lax.rem(chip + t, 16)
        return remote(
            part_send.at[c], part_recv.at[me], part_s.at[t], part_r.at[me], 2 * c, head
        )

    def start_part(t, _):
        part_copy(t).start()
        return 0

    lax.fori_loop(1, 16, start_part, 0)

    @pl.when(core == 1)
    def _():
        part_copy(0).start()

    table_ref[...] = arrival_table(split, me, dest_ref[...], slot_ref[...])
    start_second(0)

    @pl.when(core == 0)
    def _():
        part_recv[me] = part_send[chip]

        def got_part(o, _):
            src = lax.rem(me + o, INST)
            remote(
                part_send.at[0], part_recv.at[src], part_s.at[0], part_r.at[src], src, head
            ).wait_recv()
            return 0

        lax.fori_loop(1, INST, got_part, 0)
        q_group = qf[pl.ds(pl.multiple_of(chip * 8, 8), 8)].astype(jnp.bfloat16)
        attended = finish_rows(
            part_recv[...],
            chip,
            q_group,
            nk_ref[...],
            nv_ref[...].astype(jnp.float32),
            sign_row,
            rotate,
            scale,
        )
        att[chip] = attended.astype(jnp.bfloat16).astype(jnp.float32)

        def send_att(o, _):
            remote(
                att.at[chip],
                att.at[chip],
                att_s.at[o],
                att_r.at[chip],
                lax.rem(me + o, INST),
                head,
            ).start()
            return 0

        lax.fori_loop(1, INST, send_att, 0)

    start_second(1)

    def att_from(c):
        return remote(att.at[c], att.at[c], att_s.at[0], att_r.at[c], 2 * c, head)

    def got_att(t, _):
        att_from(lax.rem(chip + t, 16)).wait_recv()
        return 0

    lax.fori_loop(1, 16, got_att, 0)

    @pl.when(core == 1)
    def _():
        att_from(chip).wait_recv()

    everyone = att[...]
    terms = jnp.zeros((16, 256), jnp.float32)
    for h in range(8):
        terms = terms + jnp.dot(
            everyone[:, h, :].astype(jnp.bfloat16),
            w_ref[h * HD : (h + 1) * HD, :],
            preferred_element_type=jnp.float32,
        )
    proj[head] = terms

    def proj_copy(o):
        return remote(
            proj.at[head],
            proj.at[head],
            proj_s.at[o],
            proj_r.at[head],
            me,
            lax.rem(head + o, HEADS),
        )

    def start_proj(o, _):
        proj_copy(o).start()
        return 0

    def got_proj(o, _):
        z = lax.rem(head + o, HEADS)
        remote(proj.at[z], proj.at[z], proj_s.at[o], proj_r.at[z], me, z).wait_recv()
        return 0

    lax.fori_loop(1, HEADS, start_proj, 0)
    lax.fori_loop(1, HEADS, got_proj, 0)
    out_ref[...] = jnp.sum(proj[...], axis=0)

    def sent_proj(o, _):
        proj_copy(o).wait_send()
        return 0

    def sent_part(t, _):
        part_copy(t).wait_send()
        return 0

    lax.fori_loop(1, HEADS, sent_proj, 0)
    lax.fori_loop(1, 16, sent_part, 0)

    @pl.when(core == 1)
    def _():
        part_copy(0).wait_send()

    @pl.when(core == 0)
    def _():
        def sent_att(o, _):
            remote(
                att.at[chip],
                att.at[chip],
                att_s.at[o],
                att_r.at[chip],
                lax.rem(me + o, INST),
                head,
            ).wait_send()
            return 0

        lax.fori_loop(1, INST, sent_att, 0)

    def finish(t, _):
        d, j = t // 2, t % 2
        for half in range(2):
            for plane in range(2):

                @pl.when((d > 0) | (j != core))
                def _(plane=plane, half=half):
                    first_copy(plane, half, d, j).wait_send()
                    second_copy(plane, half, d, j).wait_send()

                second_wait(plane, half, d, j).wait()
        return 0

    lax.fori_loop(0, 8, finish, 0)


def layer_call(variant, operands):
    split, cap1, cap2 = VARIANTS[variant]
    vmem = pl.BlockSpec(memory_space=pltpu.VMEM)
    smem = pl.BlockSpec(memory_space=pltpu.SMEM)
    hbm = pl.BlockSpec(memory_space=pl.ANY)
    blocks = jax.ShapeDtypeStruct((2 * 8 * GROUP, BT, HD), jnp.bfloat16)
    dma = pltpu.SemaphoreType.DMA

    def low(*lead):
        return pltpu.VMEM((*lead, BT, HD), jnp.bfloat16)

    return pl.pallas_call(
        functools.partial(layer_kernel, split, cap1, cap2),
        out_shape=(
            jax.ShapeDtypeStruct((16, 256), jnp.float32),
            jax.ShapeDtypeStruct((8, 128), jnp.int32),
            blocks,
            blocks,
        ),
        in_specs=[vmem] * 9 + [hbm, hbm],
        out_specs=(vmem, vmem, hbm, hbm),
        scratch_shapes=[
            pltpu.VMEM((8, 128), jnp.int32),
            pltpu.SMEM((8, 128), jnp.int32),
            low(SLOTS),
            low(SLOTS),
            low(2, 2, 8, cap1),
            low(8 * GROUP),
            low(8 * GROUP),
            low(8 * GROUP),
            low(8 * GROUP),
            low(2, 2, 8, cap2),
            pltpu.VMEM((SLOTS // CHUNK, ROWS, CHUNK * BT), jnp.float32),
            pltpu.VMEM((ROWS, HD), jnp.float32),
            pltpu.VMEM((16, 8, 2 * HD), jnp.float32),
            pltpu.VMEM((INST, 8, 2 * HD), jnp.float32),
            pltpu.VMEM((16, 8, HD), jnp.float32),
            pltpu.VMEM((HEADS, 16, 256), jnp.float32),
            dma((2,)),
            dma,
            dma((2, 2, 8)),
            dma((2, 2, 8)),
            dma((2, 2, 8)),
            dma((2, 2, 8)),
            dma((16,)),
            dma((INST,)),
            dma((INST,)),
            dma((16,)),
            dma((HEADS,)),
            dma((HEADS,)),
        ],
        compiler_params=pltpu.CompilerParams(
            collective_id=variant, has_side_effects=True, vmem_limit_bytes=56 * 2**20
        ),
    )(*operands)


def place_kernel(table_ref, proj_ref, rk_ref, rv_ref, out_ref, mk_ref, mv_ref, sems):
    lands = ((rk_ref, mk_ref), (rv_ref, mv_ref))

    def place(s, _):
        for plane, (src, dst) in enumerate(lands):
            landed = table_ref[0, s]
            row = jnp.where(landed < 0, -1, landed // 128 if plane == 0 else landed % 128)

            @pl.when(row >= 0)
            def _(plane=plane, src=src, dst=dst, row=row):
                pltpu.make_async_copy(src.at[row], dst.at[s], sems.at[plane]).start()

            @pl.when(row < 0)
            def _(dst=dst):
                dst[s] = jnp.zeros((BT, HD), jnp.bfloat16)

        return 0

    lax.fori_loop(0, SLOTS, place, 0)
    out_ref[...] = proj_ref[...].astype(jnp.bfloat16)

    def settle(s, _):
        for plane, (src, dst) in enumerate(lands):
            landed = table_ref[0, s]
            row = jnp.where(landed < 0, -1, landed // 128 if plane == 0 else landed % 128)

            @pl.when(row >= 0)
            def _(plane=plane, src=src, dst=dst, row=row):
                pltpu.make_async_copy(src.at[row], dst.at[s], sems.at[plane]).wait()

        return 0

    lax.fori_loop(0, SLOTS, settle, 0)


def static_groups():
    out = []
    for (a0, a1), (b0, b1) in SPLITS:
        rows = []
        for inst in range(INST):
            x, y = inst // 8, inst // 2 % 4
            code = (x ^ (x // 2)) + 4 * (y ^ (y // 2))
            bits = [code >> b & 1 for b in range(4)]
            rows.append((bits[a0] + 2 * bits[a1], bits[b0] + 2 * bits[b1]))
        out.append(np.array(rows, np.int32).T)
    return np.stack(out)


def shards(
    query,
    new_keys,
    new_values,
    cache_keys,
    cache_values,
    signs,
    block_req,
    block_fill,
    dest_inst,
    new_slot,
    out_weight,
):
    vmem = pl.BlockSpec(memory_space=pltpu.VMEM)
    smem = pl.BlockSpec(memory_space=pltpu.SMEM)
    hbm = pl.BlockSpec(memory_space=pl.ANY)
    choice = pl.pallas_call(
        choose_kernel,
        out_shape=jax.ShapeDtypeStruct((1,), jnp.int32),
        in_specs=[smem],
        out_specs=smem,
    )(dest_inst)[0]
    operands = (
        dest_inst.reshape(16, 128),
        new_slot.reshape(16, 128),
        block_req.reshape(16, 128),
        block_fill.reshape(16, 128),
        query.reshape(ROWS, HD),
        new_keys.reshape(16, HD),
        new_values.reshape(16, HD),
        signs,
        out_weight,
        cache_keys.reshape(SLOTS, BT, HD),
        cache_values.reshape(SLOTS, BT, HD),
    )
    branches = [functools.partial(layer_call, variant) for variant in range(len(VARIANTS))]
    proj, table, got_keys, got_values = lax.switch(choice, branches, operands)
    layer_out, moved_keys, moved_values = pl.pallas_call(
        place_kernel,
        out_shape=(
            jax.ShapeDtypeStruct((16, 256), jnp.bfloat16),
            jax.ShapeDtypeStruct((SLOTS, BT, HD), jnp.bfloat16),
            jax.ShapeDtypeStruct((SLOTS, BT, HD), jnp.bfloat16),
        ),
        in_specs=[smem, vmem, hbm, hbm],
        out_specs=(vmem, vmem, vmem),
        scratch_shapes=[pltpu.SemaphoreType.DMA((2,))],
        compiler_params=pltpu.CompilerParams(vmem_limit_bytes=32 * 2**20),
    )(table, proj, got_keys, got_values)
    return (
        layer_out.reshape(2, 8, 256),
        moved_keys.reshape(SLOTS, BT, 1, HD),
        moved_values.reshape(SLOTS, BT, 1, HD),
    )


def solution(mesh):
    placed = (
        P(None, None, "head", None),
        P(None, None, "head", None),
        P(None, None, "head", None),
        P("inst", None, "head", None),
        P("inst", None, "head", None),
        P("head", None),
        P(),
        P(),
        P(),
        P(),
        P("head", "inst"),
    )
    return jax.shard_map(
        shards,
        mesh=mesh,
        in_specs=placed,
        out_specs=(
            P(None, None, "inst"),
            P("inst", None, "head", None),
            P("inst", None, "head", None),
        ),
        check_vma=False,
    )
```

```python
import functools
import math

import jax
import jax.numpy as jnp
import numpy as np
from jax import lax
from jax.experimental import pallas as pl
from jax.experimental.pallas import tpu as pltpu
from jax.sharding import PartitionSpec as P

NEG_FILL = -1e30
HIGHEST = lax.Precision.HIGHEST
MESH = pl.DeviceIdType.MESH
INST = 32
HEADS = 8
PER = 4
SLOTS = 64
BT = 128
HD = 128
ROWS = 128
CHUNK = 4
GROUP = 8
SPLITS = (((0, 1), (2, 3)), ((0, 2), (1, 3)), ((0, 3), (1, 2)))
VARIANTS = (
    (0, 5, 5),
    (1, 5, 5),
    (2, 5, 5),
    (0, 5, 6),
    (1, 5, 6),
    (2, 5, 6),
    (0, 6, 5),
    (1, 6, 5),
    (2, 6, 5),
    (0, 6, 6),
    (1, 6, 6),
    (2, 6, 6),
    (0, 7, 7),
    (0, 8, 8),
)
SEND, SOURCE, DEST, REQ, FILL = 0, 2, 4, 6, 7


def hadamard(order_size):
    common = jnp.bitwise_and(
        lax.broadcasted_iota(jnp.int32, (order_size, order_size), 0),
        lax.broadcasted_iota(jnp.int32, (order_size, order_size), 1),
    )
    parity = common
    for shift in (4, 2, 1):
        parity = jnp.bitwise_xor(parity, jnp.right_shift(parity, shift))
    return (1 - 2 * jnp.bitwise_and(parity, 1)).astype(jnp.float32)


def remote(src, dst, send_sem, recv_sem, inst, head):
    return pltpu.make_async_remote_copy(
        src_ref=src,
        dst_ref=dst,
        send_sem=send_sem,
        recv_sem=recv_sem,
        device_id=(inst, head),
        device_id_type=MESH,
    )


def attend(plan_ref, q_low, kc, vc, scores, scale):
    row_req = lax.broadcasted_iota(jnp.int32, (ROWS, BT), 0) // 8 % 8
    token = lax.broadcasted_iota(jnp.int32, (ROWS, BT), 1)
    chunks = SLOTS // CHUNK

    def score_chunk(i, top):
        keys = kc[pl.ds(i * CHUNK, CHUNK)].reshape(CHUNK * BT, HD)
        s = lax.dot_general(
            q_low, keys, (((1,), (1,)), ((), ())), preferred_element_type=jnp.float32
        )
        for c in range(CHUNK):
            req = plan_ref[REQ, i * CHUNK + c]
            fill = plan_ref[FILL, i * CHUNK + c]
            live = (row_req == req) & (token < fill)
            part = jnp.where(live, s[:, c * BT : (c + 1) * BT] * scale, NEG_FILL)
            scores[i, :, c * BT : (c + 1) * BT] = part
            top = jnp.maximum(top, part)
        return top

    top = lax.fori_loop(0, chunks, score_chunk, jnp.full((ROWS, BT), NEG_FILL, jnp.float32))
    row_max = jnp.max(top, axis=1, keepdims=True)

    def value_chunk(i, carry):
        total, acc = carry
        p = jnp.exp(scores[i] - row_max)
        for c in range(CHUNK):
            total = total + p[:, c * BT : (c + 1) * BT]
        values = vc[pl.ds(i * CHUNK, CHUNK)].reshape(CHUNK * BT, HD)
        acc = acc + jnp.dot(p.astype(jnp.bfloat16), values, preferred_element_type=jnp.float32)
        return total, acc

    zero = jnp.zeros((ROWS, BT), jnp.float32)
    total, acc = lax.fori_loop(0, chunks, value_chunk, (zero, zero))
    return row_max, jnp.sum(total, axis=1, keepdims=True), acc


def finish_rows(parts, group, q_group, nk, nv, sign_row, rotate, scale):
    req, step = group % 8, group // 8
    part_max = parts[:, :, HD : HD + 1]
    part_total = parts[:, :, HD + 64 : HD + 65]
    cache_max = jnp.max(part_max, axis=0)
    factor = jnp.exp(part_max - cache_max[None])
    cache_total = jnp.sum(part_total * factor, axis=0)
    cache_sum = jnp.sum(parts[:, :, :HD] * factor, axis=0)
    new_scores = (
        lax.dot_general(q_group, nk, (((1,), (1,)), ((), ())), preferred_element_type=jnp.float32)
        * scale
    )
    col = lax.broadcasted_iota(jnp.int32, (8, 16), 1)
    causal = (col % 8 == req) & (col // 8 <= step)
    new_scores = jnp.where(causal, new_scores, NEG_FILL)
    joined_max = jnp.maximum(cache_max, jnp.max(new_scores, axis=1, keepdims=True))
    cache_factor = jnp.exp(cache_max - joined_max)
    weights = jnp.where(causal, jnp.exp(new_scores - joined_max), 0.0)
    denominator = cache_factor * cache_total + jnp.sum(weights, axis=1, keepdims=True)
    back = jnp.dot(
        cache_factor * cache_sum, rotate, precision=HIGHEST, preferred_element_type=jnp.float32
    )
    back = back * sign_row * (1.0 / math.sqrt(HD))
    fresh = jnp.dot(weights, nv, precision=HIGHEST, preferred_element_type=jnp.float32)
    return (back + fresh) / denominator


def coordinates(inst, split):
    x, y = inst // 8, inst // 2 % 4
    code = jnp.bitwise_xor(x, x // 2) + 4 * jnp.bitwise_xor(y, y // 2)
    (a0, a1), (b0, b1) = SPLITS[split]

    def bit(b):
        return code // (1 << b) % 2

    return bit(a0) + 2 * bit(a1), bit(b0) + 2 * bit(b1), inst % 2


def instance(u, v, core, split):
    (a0, a1), (b0, b1) = SPLITS[split]
    code = (u % 2) * (1 << a0) + (u // 2) * (1 << a1) + (v % 2) * (1 << b0) + (v // 2) * (1 << b1)
    gx, gy = code % 4, code // 4
    return jnp.bitwise_xor(gx, gx // 2) * 8 + jnp.bitwise_xor(gy, gy // 2) * 2 + core


def lanes_to_rows(row, count):
    sub = lax.broadcasted_iota(jnp.int32, (count, 128), 0)
    lane = lax.broadcasted_iota(jnp.int32, (count, 128), 1)
    return jnp.sum(jnp.where(sub == lane, row, 0), axis=1, keepdims=True)


def moved_elements(dest):
    sub = lax.broadcasted_iota(jnp.int32, (16, 128), 0)
    lane = lax.broadcasted_iota(jnp.int32, (16, 128), 1)
    return (dest != 2 * sub + lane // 64).astype(jnp.int32)


def released_row(dest):
    moved = moved_elements(dest)
    sub = lax.broadcasted_iota(jnp.int32, (16, 128), 0)
    lane = lax.broadcasted_iota(jnp.int32, (16, 128), 1)
    pick = jnp.where(lane % 2 == 0, moved[:, 0:1], moved[:, 64:65])
    return jnp.sum(jnp.where(lane // 2 == sub, pick, 0), axis=0, keepdims=True)


def own_half(ref, me):
    row = ref[pl.ds(me // 2, 1), :]
    return jnp.where(me % 2 == 1, jnp.concatenate([row[:, 64:], row[:, :64]], axis=1), row)


def write_plan(split, me, dest_ref, req_ref, fill_ref, plan):
    dest = dest_ref[...]
    sub = lax.broadcasted_iota(jnp.int32, (32, 128), 0)
    lane = lax.broadcasted_iota(jnp.int32, (32, 128), 1)
    sub_all = lax.broadcasted_iota(jnp.int32, (128, 128), 0)
    lane_all = lax.broadcasted_iota(jnp.int32, (128, 128), 1)
    gone_row = released_row(dest)
    kept_row = jnp.where(lane[:1] < INST, 1 - gone_row, 0)
    gone = lanes_to_rows(gone_row, 32)
    at_row = coordinates(lane, split)
    at_col = coordinates(sub, split)
    at_me = coordinates(me, split)
    own = own_half(dest_ref, me)
    own_col = lanes_to_rows(own, 128)
    rank = jnp.sum(
        ((own_col == own) & (sub_all < lane_all)).astype(jnp.int32), axis=0, keepdims=True
    )
    for plane in range(2):
        one, two = plane, 1 - plane
        kept_rank = jnp.sum(
            jnp.where((at_col[one] == at_row[one]) & (lane < sub), kept_row, 0),
            axis=1,
            keepdims=True,
        )
        gone_rank = jnp.sum(
            jnp.where((at_col[two] == at_row[two]) & (lane < sub), gone_row, 0),
            axis=1,
            keepdims=True,
        )
        place = at_col[one] * 32 + kept_rank * PER
        at = jnp.sum(jnp.where(sub == own, place, 0), axis=0, keepdims=True) + rank
        at = jnp.where(lane[:1] < SLOTS, at, -1)
        hit = lanes_to_rows(at, 128) == lane_all
        plan[SEND + plane : SEND + plane + 1] = jnp.sum(
            jnp.where(hit, sub_all, 0), axis=0, keepdims=True
        )
        source = (jnp.bitwise_xor(at_col[one], at_me[one]) * 2 + at_col[2]) * GROUP
        take = (gone == 1) & (at_col[two] == at_me[two]) & (gone_rank == lane)
        plan[SOURCE + plane : SOURCE + plane + 1] = jnp.sum(
            jnp.where(take, source, 0), axis=0, keepdims=True
        )
        distance = jnp.bitwise_xor(at_col[two], at_me[two]) * 2 + at_col[2]
        take = (at_col[one] == at_me[one]) & (distance == lane)
        plan[DEST + plane : DEST + plane + 1] = jnp.sum(
            jnp.where(take, kept_rank, 0), axis=0, keepdims=True
        )
    plan[REQ : REQ + 1] = own_half(req_ref, me)
    plan[FILL : FILL + 1] = own_half(fill_ref, me)


def arrival_table(split, me, dest, slot):
    sub = lax.broadcasted_iota(jnp.int32, (16, 128), 0)
    lane = lax.broadcasted_iota(jnp.int32, (16, 128), 1)
    source = 2 * sub + lane // 64
    to_me = (dest == me) & (moved_elements(dest) == 1)
    count = to_me.astype(jnp.int32)
    for step in (1, 2, 4, 8, 16, 32):
        shifted = jnp.concatenate([count[:, 128 - step :], count[:, : 128 - step]], axis=1)
        count = count + jnp.where(lane % 64 >= step, shifted, 0)
    rank = count - 1
    gone_row = released_row(dest)
    at_row = coordinates(lane, split)
    at_me = coordinates(me, split)
    landed = jnp.zeros((16, 128), jnp.int32)
    for plane in range(2):
        two = 1 - plane
        ranks = []
        for core in range(2):
            inst = 2 * sub + core
            same = (coordinates(inst, split)[two] == at_row[two]) & (lane < inst)
            ranks.append(jnp.sum(jnp.where(same, gone_row, 0), axis=1, keepdims=True))
        gone_rank = jnp.where(lane < 64, ranks[0], ranks[1])
        far = jnp.bitwise_xor(coordinates(source, split)[two], at_me[two])
        row = far * 2 * GROUP + gone_rank + rank // 2 * GROUP + rank % 2 * 8 * GROUP
        landed = landed * 128 + row
    landed = jnp.where(to_me, landed, -1)
    want = lax.broadcasted_iota(jnp.int32, (SLOTS, 128), 0)
    found = jnp.full((SLOTS, 128), -1, jnp.int32)
    for i in range(16):
        found = jnp.maximum(
            found, jnp.where(slot[i : i + 1] == want, landed[i : i + 1], -1)
        )
    column = jnp.max(found, axis=1, keepdims=True)
    spread = jnp.where(want == lax.broadcasted_iota(jnp.int32, (SLOTS, 128), 1), column + 1, 0)
    return jnp.broadcast_to(jnp.sum(spread, axis=0, keepdims=True) - 1, (8, 128))


def choose_kernel(dest_ref, choice_ref):
    gone = [(dest_ref[inst * SLOTS] != inst).astype(jnp.int32) for inst in range(INST)]
    groups = static_groups()
    need = []
    for split in range(len(SPLITS)):
        counts = []
        for coord in range(2):
            for group in range(4):
                members = [gone[i] for i in range(INST) if groups[split][coord][i] == group]
                counts.append(functools.reduce(jnp.add, members))
        most = functools.reduce(jnp.maximum, counts)
        least = functools.reduce(jnp.minimum, counts)
        need.append((8 - least, most))
    choice = jnp.full((), len(VARIANTS) - 1, jnp.int32)
    for index in reversed(range(len(VARIANTS) - 1)):
        split, cap1, cap2 = VARIANTS[index]
        fits = (need[split][0] <= cap1) & (need[split][1] <= cap2)
        choice = jnp.where(fits, index, choice)
    choice_ref[0] = choice


def layer_kernel(split, cap1, cap2, *refs):
    (
        dest_ref,
        slot_ref,
        req_ref,
        fill_ref,
        q_ref,
        nk_ref,
        nv_ref,
        signs_ref,
        w_ref,
        ck_ref,
        cv_ref,
        out_ref,
        table_ref,
        rk_ref,
        rv_ref,
        plan_vmem,
        plan_ref,
        kc,
        vc,
        first_send,
        mid_k0,
        mid_k1,
        mid_v0,
        mid_v1,
        second_send,
        scores,
        qf,
        part_send,
        part_recv,
        att,
        proj,
        load_sem,
        plan_sem,
        first_s,
        first_r,
        second_s,
        second_r,
        part_s,
        part_r,
        att_s,
        att_r,
        proj_s,
        proj_r,
    ) = refs
    me = lax.axis_index("inst")
    head = lax.axis_index("head")
    chip, core = me // 2, me % 2
    u, v, _ = coordinates(me, split)
    scale = 1.0 / math.sqrt(HD)
    caches = (kc, vc)
    mids = ((mid_k0, mid_k1), (mid_v0, mid_v1))
    lands = (rk_ref, rv_ref)

    load_k = pltpu.make_async_copy(ck_ref, kc, load_sem.at[0])
    load_v = pltpu.make_async_copy(cv_ref, vc, load_sem.at[1])
    load_k.start()
    load_v.start()

    barrier = pltpu.get_barrier_semaphore()

    def greet_inst(o, _):
        pl.semaphore_signal(
            barrier, inc=1, device_id=(lax.rem(me + o, INST), head), device_id_type=MESH
        )
        return 0

    def greet_head(o, _):
        pl.semaphore_signal(
            barrier, inc=1, device_id=(me, lax.rem(head + o, HEADS)), device_id_type=MESH
        )
        return 0

    lax.fori_loop(1, HEADS, greet_head, 0)
    lax.fori_loop(1, INST, greet_inst, 0)

    write_plan(split, me, dest_ref, req_ref, fill_ref, plan_vmem)
    to_smem = pltpu.make_async_copy(plan_vmem, plan_ref, plan_sem)
    to_smem.start()

    sign_row = (2 * signs_ref[...] - 1).astype(jnp.float32)
    rotate = hadamard(HD)
    raw = q_ref[...].astype(jnp.float32)
    qf[...] = raw
    q_rot = jnp.dot(
        (raw * sign_row).astype(jnp.bfloat16),
        rotate.astype(jnp.bfloat16),
        preferred_element_type=jnp.float32,
    ) * (1.0 / math.sqrt(HD))
    q_low = q_rot.astype(jnp.bfloat16)

    to_smem.wait()
    load_k.wait()
    load_v.wait()
    pl.semaphore_wait(barrier, INST - 1 + HEADS - 1)

    def peer(plane, along_first, d, j):
        if (plane == 0) == along_first:
            return instance(jnp.bitwise_xor(u, d), v, j, split)
        return instance(u, jnp.bitwise_xor(v, d), j, split)

    def first_copy(plane, half, d, j):
        src = first_send.at[plane, half, d * 2 + j]
        dst = mids[plane][half].at[pl.ds((d * 2 + core) * GROUP, cap1)]
        sems = first_s.at[plane, half, d * 2 + j], first_r.at[plane, half, d * 2 + core]
        return remote(src, dst, *sems, peer(plane, True, d, j), head)

    def first_keep(plane, half):
        return pltpu.make_async_copy(
            first_send.at[plane, half, core],
            mids[plane][half].at[pl.ds(core * GROUP, cap1)],
            first_r.at[plane, half, core],
        )

    def first_wait(plane, half, d, j):
        dst = mids[plane][half].at[pl.ds((d * 2 + j) * GROUP, cap1)]
        return pltpu.make_async_copy(dst, dst, first_r.at[plane, half, d * 2 + j])

    def second_copy(plane, half, d, j):
        src = second_send.at[plane, half, d * 2 + j]
        dst = lands[plane].at[pl.ds((half * 8 + d * 2 + core) * GROUP, cap2)]
        sems = second_s.at[plane, half, d * 2 + j], second_r.at[plane, half, d * 2 + core]
        return remote(src, dst, *sems, peer(plane, False, d, j), head)

    def second_keep(plane, half):
        return pltpu.make_async_copy(
            second_send.at[plane, half, core],
            lands[plane].at[pl.ds((half * 8 + core) * GROUP, cap2)],
            second_r.at[plane, half, core],
        )

    def second_wait(plane, half, d, j):
        dst = lands[plane].at[pl.ds((half * 8 + d * 2 + j) * GROUP, cap2)]
        return pltpu.make_async_copy(dst, dst, second_r.at[plane, half, d * 2 + j])

    def start_first(half):
        def body(t, _):
            d, j = 3 - t // 2, t % 2
            for plane in range(2):
                first = jnp.bitwise_xor(u if plane == 0 else v, d)
                for m in range(cap1):
                    b = plan_ref[SEND + plane, first * 32 + m * PER + j * 2 + half]
                    first_send[plane, half, d * 2 + j, m] = caches[plane][b]

                @pl.when((d > 0) | (j != core))
                def _(plane=plane):
                    first_copy(plane, half, d, j).start()

                @pl.when((d == 0) & (j == core))
                def _(plane=plane):
                    first_keep(plane, half).start()

            return 0

        lax.fori_loop(0, 8, body, 0)

    def start_second(half):
        def wait_body(t, _):
            for plane in range(2):
                first_wait(plane, half, t // 2, t % 2).wait()
            return 0

        lax.fori_loop(0, 8, wait_body, 0)

        def body(t, _):
            d, j = 3 - t // 2, t % 2
            for plane in range(2):
                base = plan_ref[DEST + plane, d * 2 + j]
                for n in range(cap2):
                    b = base + plan_ref[SOURCE + plane, n]
                    second_send[plane, half, d * 2 + j, n] = mids[plane][half][b]

                @pl.when((d > 0) | (j != core))
                def _(plane=plane):
                    second_copy(plane, half, d, j).start()

                @pl.when((d == 0) & (j == core))
                def _(plane=plane):
                    second_keep(plane, half).start()

            return 0

        lax.fori_loop(0, 8, body, 0)

    start_first(0)
    start_first(1)

    row_max, row_total, acc = attend(plan_ref, q_low, kc, vc, scores, scale)
    lane = lax.broadcasted_iota(jnp.int32, (ROWS, HD), 1)
    part_send[:, :, :HD] = acc.reshape(16, 8, HD)
    part_send[:, :, HD:] = jnp.where(lane < 64, row_max, row_total).reshape(16, 8, HD)

    def part_copy(t):
        c = lax.rem(chip + t, 16)
        return remote(
            part_send.at[c], part_recv.at[me], part_s.at[t], part_r.at[me], 2 * c, head
        )

    def start_part(t, _):
        part_copy(t).start()
        return 0

    lax.fori_loop(1, 16, start_part, 0)

    @pl.when(core == 1)
    def _():
        part_copy(0).start()

    table_ref[...] = arrival_table(split, me, dest_ref[...], slot_ref[...])
    start_second(0)

    @pl.when(core == 0)
    def _():
        part_recv[me] = part_send[chip]

        def got_part(o, _):
            src = lax.rem(me + o, INST)
            remote(
                part_send.at[0], part_recv.at[src], part_s.at[0], part_r.at[src], src, head
            ).wait_recv()
            return 0

        lax.fori_loop(1, INST, got_part, 0)
        q_group = qf[pl.ds(pl.multiple_of(chip * 8, 8), 8)].astype(jnp.bfloat16)
        attended = finish_rows(
            part_recv[...],
            chip,
            q_group,
            nk_ref[...],
            nv_ref[...].astype(jnp.float32),
            sign_row,
            rotate,
            scale,
        )
        att[chip] = attended.astype(jnp.bfloat16).astype(jnp.float32)

        def send_att(o, _):
            remote(
                att.at[chip],
                att.at[chip],
                att_s.at[o],
                att_r.at[chip],
                lax.rem(me + o, INST),
                head,
            ).start()
            return 0

        lax.fori_loop(1, INST, send_att, 0)

    start_second(1)

    def att_from(c):
        return remote(att.at[c], att.at[c], att_s.at[0], att_r.at[c], 2 * c, head)

    def got_att(t, _):
        att_from(lax.rem(chip + t, 16)).wait_recv()
        return 0

    lax.fori_loop(1, 16, got_att, 0)

    @pl.when(core == 1)
    def _():
        att_from(chip).wait_recv()

    everyone = att[...]
    terms = jnp.zeros((16, 256), jnp.float32)
    for h in range(8):
        terms = terms + jnp.dot(
            everyone[:, h, :].astype(jnp.bfloat16),
            w_ref[h * HD : (h + 1) * HD, :],
            preferred_element_type=jnp.float32,
        )
    proj[head] = terms

    def proj_copy(o):
        return remote(
            proj.at[head],
            proj.at[head],
            proj_s.at[o],
            proj_r.at[head],
            me,
            lax.rem(head + o, HEADS),
        )

    def start_proj(o, _):
        proj_copy(o).start()
        return 0

    def got_proj(o, _):
        z = lax.rem(head + o, HEADS)
        remote(proj.at[z], proj.at[z], proj_s.at[o], proj_r.at[z], me, z).wait_recv()
        return 0

    lax.fori_loop(1, HEADS, start_proj, 0)
    lax.fori_loop(1, HEADS, got_proj, 0)
    out_ref[...] = jnp.sum(proj[...], axis=0)

    def sent_proj(o, _):
        proj_copy(o).wait_send()
        return 0

    def sent_part(t, _):
        part_copy(t).wait_send()
        return 0

    lax.fori_loop(1, HEADS, sent_proj, 0)
    lax.fori_loop(1, 16, sent_part, 0)

    @pl.when(core == 1)
    def _():
        part_copy(0).wait_send()

    @pl.when(core == 0)
    def _():
        def sent_att(o, _):
            remote(
                att.at[chip],
                att.at[chip],
                att_s.at[o],
                att_r.at[chip],
                lax.rem(me + o, INST),
                head,
            ).wait_send()
            return 0

        lax.fori_loop(1, INST, sent_att, 0)

    def finish(t, _):
        d, j = t // 2, t % 2
        for half in range(2):
            for plane in range(2):

                @pl.when((d > 0) | (j != core))
                def _(plane=plane, half=half):
                    first_copy(plane, half, d, j).wait_send()
                    second_copy(plane, half, d, j).wait_send()

                second_wait(plane, half, d, j).wait()
        return 0

    lax.fori_loop(0, 8, finish, 0)


def layer_call(variant, operands):
    split, cap1, cap2 = VARIANTS[variant]
    vmem = pl.BlockSpec(memory_space=pltpu.VMEM)
    smem = pl.BlockSpec(memory_space=pltpu.SMEM)
    hbm = pl.BlockSpec(memory_space=pl.ANY)
    blocks = jax.ShapeDtypeStruct((2 * 8 * GROUP, BT, HD), jnp.bfloat16)
    dma = pltpu.SemaphoreType.DMA

    def low(*lead):
        return pltpu.VMEM((*lead, BT, HD), jnp.bfloat16)

    return pl.pallas_call(
        functools.partial(layer_kernel, split, cap1, cap2),
        out_shape=(
            jax.ShapeDtypeStruct((16, 256), jnp.float32),
            jax.ShapeDtypeStruct((8, 128), jnp.int32),
            blocks,
            blocks,
        ),
        in_specs=[vmem] * 9 + [hbm, hbm],
        out_specs=(vmem, vmem, hbm, hbm),
        scratch_shapes=[
            pltpu.VMEM((8, 128), jnp.int32),
            pltpu.SMEM((8, 128), jnp.int32),
            low(SLOTS),
            low(SLOTS),
            low(2, 2, 8, cap1),
            low(8 * GROUP),
            low(8 * GROUP),
            low(8 * GROUP),
            low(8 * GROUP),
            low(2, 2, 8, cap2),
            pltpu.VMEM((SLOTS // CHUNK, ROWS, CHUNK * BT), jnp.float32),
            pltpu.VMEM((ROWS, HD), jnp.float32),
            pltpu.VMEM((16, 8, 2 * HD), jnp.float32),
            pltpu.VMEM((INST, 8, 2 * HD), jnp.float32),
            pltpu.VMEM((16, 8, HD), jnp.float32),
            pltpu.VMEM((HEADS, 16, 256), jnp.float32),
            dma((2,)),
            dma,
            dma((2, 2, 8)),
            dma((2, 2, 8)),
            dma((2, 2, 8)),
            dma((2, 2, 8)),
            dma((16,)),
            dma((INST,)),
            dma((INST,)),
            dma((16,)),
            dma((HEADS,)),
            dma((HEADS,)),
        ],
        compiler_params=pltpu.CompilerParams(
            collective_id=variant, has_side_effects=True, vmem_limit_bytes=56 * 2**20
        ),
    )(*operands)


def place_kernel(
    table_ref, proj_ref, rk_ref, rv_ref, out_ref, mk_ref, mv_ref, placed, in_sems, out_sems
):
    lands = ((rk_ref, mk_ref), (rv_ref, mv_ref))
    parts, width = 4, SLOTS // 4

    def store(plane, src_plane, part):
        rows = pl.ds(part * width, width)
        return pltpu.make_async_copy(
            placed.at[src_plane, rows], lands[plane][1].at[rows], out_sems.at[plane, part]
        )

    kept = table_ref[0, 0] >= 0

    @pl.when(kept)
    def _():
        for part in range(parts):

            def fetch(t, _):
                s = part * width + t
                landed = table_ref[0, s]
                for plane, row in enumerate((landed // 128, landed % 128)):
                    pltpu.make_async_copy(
                        lands[plane][0].at[row], placed.at[plane, s], in_sems.at[plane, part]
                    ).start()
                return 0

            lax.fori_loop(0, width, fetch, 0, unroll=4)
        for part in range(parts):
            rows = pl.ds(part * width, width)
            for plane in range(2):
                pltpu.make_async_copy(
                    lands[plane][0].at[rows], placed.at[plane, rows], in_sems.at[plane, part]
                ).wait()
                store(plane, plane, part).start()

    @pl.when(jnp.logical_not(kept))
    def _():
        placed[0, :width] = jnp.zeros((width, BT, HD), jnp.bfloat16)
        for plane in range(2):
            for part in range(parts):
                rows = pl.ds(part * width, width)
                pltpu.make_async_copy(
                    placed.at[0, pl.ds(0, width)], lands[plane][1].at[rows], out_sems.at[plane, part]
                ).start()

    out_ref[...] = proj_ref[...].astype(jnp.bfloat16)
    for plane in range(2):
        for part in range(parts):
            store(plane, plane, part).wait()


def static_groups():
    out = []
    for (a0, a1), (b0, b1) in SPLITS:
        rows = []
        for inst in range(INST):
            x, y = inst // 8, inst // 2 % 4
            code = (x ^ (x // 2)) + 4 * (y ^ (y // 2))
            bits = [code >> b & 1 for b in range(4)]
            rows.append((bits[a0] + 2 * bits[a1], bits[b0] + 2 * bits[b1]))
        out.append(np.array(rows, np.int32).T)
    return np.stack(out)


def shards(
    query,
    new_keys,
    new_values,
    cache_keys,
    cache_values,
    signs,
    block_req,
    block_fill,
    dest_inst,
    new_slot,
    out_weight,
):
    vmem = pl.BlockSpec(memory_space=pltpu.VMEM)
    smem = pl.BlockSpec(memory_space=pltpu.SMEM)
    hbm = pl.BlockSpec(memory_space=pl.ANY)
    choice = pl.pallas_call(
        choose_kernel,
        out_shape=jax.ShapeDtypeStruct((1,), jnp.int32),
        in_specs=[smem],
        out_specs=smem,
    )(dest_inst)[0]
    operands = (
        dest_inst.reshape(16, 128),
        new_slot.reshape(16, 128),
        block_req.reshape(16, 128),
        block_fill.reshape(16, 128),
        query.reshape(ROWS, HD),
        new_keys.reshape(16, HD),
        new_values.reshape(16, HD),
        signs,
        out_weight,
        cache_keys.reshape(SLOTS, BT, HD),
        cache_values.reshape(SLOTS, BT, HD),
    )
    branches = [functools.partial(layer_call, variant) for variant in range(len(VARIANTS))]
    proj, table, got_keys, got_values = lax.switch(choice, branches, operands)
    layer_out, moved_keys, moved_values = pl.pallas_call(
        place_kernel,
        out_shape=(
            jax.ShapeDtypeStruct((16, 256), jnp.bfloat16),
            jax.ShapeDtypeStruct((SLOTS, BT, HD), jnp.bfloat16),
            jax.ShapeDtypeStruct((SLOTS, BT, HD), jnp.bfloat16),
        ),
        in_specs=[smem, vmem, hbm, hbm],
        out_specs=(vmem, hbm, hbm),
        scratch_shapes=[
            pltpu.VMEM((2, SLOTS, BT, HD), jnp.bfloat16),
            pltpu.SemaphoreType.DMA((2, 4)),
            pltpu.SemaphoreType.DMA((2, 4)),
        ],
        compiler_params=pltpu.CompilerParams(vmem_limit_bytes=32 * 2**20),
    )(
        table,
        proj,
        got_keys,
        got_values,
    )
    return (
        layer_out.reshape(2, 8, 256),
        moved_keys.reshape(SLOTS, BT, 1, HD),
        moved_values.reshape(SLOTS, BT, 1, HD),
    )


def solution(mesh):
    placed = (
        P(None, None, "head", None),
        P(None, None, "head", None),
        P(None, None, "head", None),
        P("inst", None, "head", None),
        P("inst", None, "head", None),
        P("head", None),
        P(),
        P(),
        P(),
        P(),
        P("head", "inst"),
    )
    return jax.shard_map(
        shards,
        mesh=mesh,
        in_specs=placed,
        out_specs=(
            P(None, None, "inst"),
            P("inst", None, "head", None),
            P("inst", None, "head", None),
        ),
        check_vma=False,
    )
```

```python
import functools
import math

import jax
import jax.numpy as jnp
import numpy as np
from jax import lax
from jax.experimental import pallas as pl
from jax.experimental.pallas import tpu as pltpu
from jax.sharding import PartitionSpec as P

NEG_FILL = -1e30
HIGHEST = lax.Precision.HIGHEST
MESH = pl.DeviceIdType.MESH
INST = 32
HEADS = 8
PER = 4
SLOTS = 64
BT = 128
HD = 128
ROWS = 128
CHUNK = 4
GROUP = 8
SPLITS = (((0, 1), (2, 3)), ((0, 2), (1, 3)), ((0, 3), (1, 2)))
VARIANTS = (
    (0, 5, 5),
    (1, 5, 5),
    (2, 5, 5),
    (0, 5, 6),
    (1, 5, 6),
    (2, 5, 6),
    (0, 6, 5),
    (1, 6, 5),
    (2, 6, 5),
    (0, 6, 6),
    (1, 6, 6),
    (2, 6, 6),
    (0, 7, 7),
    (0, 8, 8),
)
SEND, SOURCE, DEST, REQ, FILL = 0, 2, 4, 6, 7


def hadamard(order_size):
    common = jnp.bitwise_and(
        lax.broadcasted_iota(jnp.int32, (order_size, order_size), 0),
        lax.broadcasted_iota(jnp.int32, (order_size, order_size), 1),
    )
    parity = common
    for shift in (4, 2, 1):
        parity = jnp.bitwise_xor(parity, jnp.right_shift(parity, shift))
    return (1 - 2 * jnp.bitwise_and(parity, 1)).astype(jnp.float32)


def remote(src, dst, send_sem, recv_sem, inst, head):
    return pltpu.make_async_remote_copy(
        src_ref=src,
        dst_ref=dst,
        send_sem=send_sem,
        recv_sem=recv_sem,
        device_id=(inst, head),
        device_id_type=MESH,
    )


def attend(plan_ref, q_low, kc, vc, scores, scale):
    row_req = lax.broadcasted_iota(jnp.int32, (ROWS, BT), 0) // 8 % 8
    token = lax.broadcasted_iota(jnp.int32, (ROWS, BT), 1)
    chunks = SLOTS // CHUNK

    def score_chunk(i, top):
        keys = kc[pl.ds(i * CHUNK, CHUNK)].reshape(CHUNK * BT, HD)
        s = lax.dot_general(
            q_low, keys, (((1,), (1,)), ((), ())), preferred_element_type=jnp.float32
        )
        for c in range(CHUNK):
            req = plan_ref[REQ, i * CHUNK + c]
            fill = plan_ref[FILL, i * CHUNK + c]
            live = (row_req == req) & (token < fill)
            part = jnp.where(live, s[:, c * BT : (c + 1) * BT] * scale, NEG_FILL)
            scores[i, :, c * BT : (c + 1) * BT] = part
            top = jnp.maximum(top, part)
        return top

    top = lax.fori_loop(0, chunks, score_chunk, jnp.full((ROWS, BT), NEG_FILL, jnp.float32))
    row_max = jnp.max(top, axis=1, keepdims=True)

    def value_chunk(i, carry):
        total, acc = carry
        p = jnp.exp(scores[i] - row_max)
        for c in range(CHUNK):
            total = total + p[:, c * BT : (c + 1) * BT]
        values = vc[pl.ds(i * CHUNK, CHUNK)].reshape(CHUNK * BT, HD)
        acc = acc + jnp.dot(p.astype(jnp.bfloat16), values, preferred_element_type=jnp.float32)
        return total, acc

    zero = jnp.zeros((ROWS, BT), jnp.float32)
    total, acc = lax.fori_loop(0, chunks, value_chunk, (zero, zero))
    return row_max, jnp.sum(total, axis=1, keepdims=True), acc


def joined_pair(one, two):
    max_one, max_two = one[:, :, HD : HD + 1], two[:, :, HD : HD + 1]
    joined_max = jnp.maximum(max_one, max_two)
    joined = one * jnp.exp(max_one - joined_max) + two * jnp.exp(max_two - joined_max)
    lane = lax.broadcasted_iota(jnp.int32, one.shape, 2)
    return jnp.where((lane >= HD) & (lane < HD + 64), joined_max, joined)


def finish_rows(parts, group, q_group, nk, nv, sign_row, rotate, scale):
    req, step = group % 8, group // 8
    part_max = parts[:, :, HD : HD + 1]
    part_total = parts[:, :, HD + 64 : HD + 65]
    cache_max = jnp.max(part_max, axis=0)
    factor = jnp.exp(part_max - cache_max[None])
    cache_total = jnp.sum(part_total * factor, axis=0)
    cache_sum = jnp.sum(parts[:, :, :HD] * factor, axis=0)
    new_scores = (
        lax.dot_general(q_group, nk, (((1,), (1,)), ((), ())), preferred_element_type=jnp.float32)
        * scale
    )
    col = lax.broadcasted_iota(jnp.int32, (8, 16), 1)
    causal = (col % 8 == req) & (col // 8 <= step)
    new_scores = jnp.where(causal, new_scores, NEG_FILL)
    joined_max = jnp.maximum(cache_max, jnp.max(new_scores, axis=1, keepdims=True))
    cache_factor = jnp.exp(cache_max - joined_max)
    weights = jnp.where(causal, jnp.exp(new_scores - joined_max), 0.0)
    denominator = cache_factor * cache_total + jnp.sum(weights, axis=1, keepdims=True)
    back = jnp.dot(
        cache_factor * cache_sum, rotate, precision=HIGHEST, preferred_element_type=jnp.float32
    )
    back = back * sign_row * (1.0 / math.sqrt(HD))
    fresh = jnp.dot(weights, nv, precision=HIGHEST, preferred_element_type=jnp.float32)
    return (back + fresh) / denominator


def coordinates(inst, split):
    x, y = inst // 8, inst // 2 % 4
    code = jnp.bitwise_xor(x, x // 2) + 4 * jnp.bitwise_xor(y, y // 2)
    (a0, a1), (b0, b1) = SPLITS[split]

    def bit(b):
        return code // (1 << b) % 2

    return bit(a0) + 2 * bit(a1), bit(b0) + 2 * bit(b1), inst % 2


def instance(u, v, core, split):
    (a0, a1), (b0, b1) = SPLITS[split]
    code = (u % 2) * (1 << a0) + (u // 2) * (1 << a1) + (v % 2) * (1 << b0) + (v // 2) * (1 << b1)
    gx, gy = code % 4, code // 4
    return jnp.bitwise_xor(gx, gx // 2) * 8 + jnp.bitwise_xor(gy, gy // 2) * 2 + core


def lanes_to_rows(row, count):
    sub = lax.broadcasted_iota(jnp.int32, (count, 128), 0)
    lane = lax.broadcasted_iota(jnp.int32, (count, 128), 1)
    return jnp.sum(jnp.where(sub == lane, row, 0), axis=1, keepdims=True)


def moved_elements(dest):
    sub = lax.broadcasted_iota(jnp.int32, (16, 128), 0)
    lane = lax.broadcasted_iota(jnp.int32, (16, 128), 1)
    return (dest != 2 * sub + lane // 64).astype(jnp.int32)


def released_row(dest):
    moved = moved_elements(dest)
    sub = lax.broadcasted_iota(jnp.int32, (16, 128), 0)
    lane = lax.broadcasted_iota(jnp.int32, (16, 128), 1)
    pick = jnp.where(lane % 2 == 0, moved[:, 0:1], moved[:, 64:65])
    return jnp.sum(jnp.where(lane // 2 == sub, pick, 0), axis=0, keepdims=True)


def own_half(ref, me):
    row = ref[pl.ds(me // 2, 1), :]
    return jnp.where(me % 2 == 1, jnp.concatenate([row[:, 64:], row[:, :64]], axis=1), row)


def write_plan(split, me, dest_ref, req_ref, fill_ref, plan):
    dest = dest_ref[...]
    sub = lax.broadcasted_iota(jnp.int32, (32, 128), 0)
    lane = lax.broadcasted_iota(jnp.int32, (32, 128), 1)
    sub_all = lax.broadcasted_iota(jnp.int32, (128, 128), 0)
    lane_all = lax.broadcasted_iota(jnp.int32, (128, 128), 1)
    gone_row = released_row(dest)
    kept_row = jnp.where(lane[:1] < INST, 1 - gone_row, 0)
    gone = lanes_to_rows(gone_row, 32)
    at_row = coordinates(lane, split)
    at_col = coordinates(sub, split)
    at_me = coordinates(me, split)
    own = own_half(dest_ref, me)
    own_col = lanes_to_rows(own, 128)
    rank = jnp.sum(
        ((own_col == own) & (sub_all < lane_all)).astype(jnp.int32), axis=0, keepdims=True
    )
    for plane in range(2):
        one, two = plane, 1 - plane
        kept_rank = jnp.sum(
            jnp.where((at_col[one] == at_row[one]) & (lane < sub), kept_row, 0),
            axis=1,
            keepdims=True,
        )
        gone_rank = jnp.sum(
            jnp.where((at_col[two] == at_row[two]) & (lane < sub), gone_row, 0),
            axis=1,
            keepdims=True,
        )
        place = at_col[one] * 32 + kept_rank * PER
        at = jnp.sum(jnp.where(sub == own, place, 0), axis=0, keepdims=True) + rank
        at = jnp.where(lane[:1] < SLOTS, at, -1)
        hit = lanes_to_rows(at, 128) == lane_all
        plan[SEND + plane : SEND + plane + 1] = jnp.sum(
            jnp.where(hit, sub_all, 0), axis=0, keepdims=True
        )
        source = (jnp.bitwise_xor(at_col[one], at_me[one]) * 2 + at_col[2]) * GROUP
        take = (gone == 1) & (at_col[two] == at_me[two]) & (gone_rank == lane)
        plan[SOURCE + plane : SOURCE + plane + 1] = jnp.sum(
            jnp.where(take, source, 0), axis=0, keepdims=True
        )
        distance = jnp.bitwise_xor(at_col[two], at_me[two]) * 2 + at_col[2]
        take = (at_col[one] == at_me[one]) & (distance == lane)
        plan[DEST + plane : DEST + plane + 1] = jnp.sum(
            jnp.where(take, kept_rank, 0), axis=0, keepdims=True
        )
    plan[REQ : REQ + 1] = own_half(req_ref, me)
    plan[FILL : FILL + 1] = own_half(fill_ref, me)


def arrival_table(split, me, dest, slot):
    sub = lax.broadcasted_iota(jnp.int32, (16, 128), 0)
    lane = lax.broadcasted_iota(jnp.int32, (16, 128), 1)
    source = 2 * sub + lane // 64
    to_me = (dest == me) & (moved_elements(dest) == 1)
    count = to_me.astype(jnp.int32)
    for step in (1, 2, 4, 8, 16, 32):
        shifted = jnp.concatenate([count[:, 128 - step :], count[:, : 128 - step]], axis=1)
        count = count + jnp.where(lane % 64 >= step, shifted, 0)
    rank = count - 1
    gone_row = released_row(dest)
    at_row = coordinates(lane, split)
    at_me = coordinates(me, split)
    landed = jnp.zeros((16, 128), jnp.int32)
    for plane in range(2):
        two = 1 - plane
        ranks = []
        for core in range(2):
            inst = 2 * sub + core
            same = (coordinates(inst, split)[two] == at_row[two]) & (lane < inst)
            ranks.append(jnp.sum(jnp.where(same, gone_row, 0), axis=1, keepdims=True))
        gone_rank = jnp.where(lane < 64, ranks[0], ranks[1])
        far = jnp.bitwise_xor(coordinates(source, split)[two], at_me[two])
        row = far * 2 * GROUP + gone_rank + rank // 2 * GROUP + rank % 2 * 8 * GROUP
        landed = landed * 128 + row
    landed = jnp.where(to_me, landed, -1)
    want = lax.broadcasted_iota(jnp.int32, (SLOTS, 128), 0)
    found = jnp.full((SLOTS, 128), -1, jnp.int32)
    for i in range(16):
        found = jnp.maximum(
            found, jnp.where(slot[i : i + 1] == want, landed[i : i + 1], -1)
        )
    column = jnp.max(found, axis=1, keepdims=True)
    spread = jnp.where(want == lax.broadcasted_iota(jnp.int32, (SLOTS, 128), 1), column + 1, 0)
    return jnp.broadcast_to(jnp.sum(spread, axis=0, keepdims=True) - 1, (8, 128))


def choose_kernel(dest_ref, choice_ref):
    gone = [(dest_ref[inst * SLOTS] != inst).astype(jnp.int32) for inst in range(INST)]
    groups = static_groups()
    need = []
    for split in range(len(SPLITS)):
        counts = []
        for coord in range(2):
            for group in range(4):
                members = [gone[i] for i in range(INST) if groups[split][coord][i] == group]
                counts.append(functools.reduce(jnp.add, members))
        most = functools.reduce(jnp.maximum, counts)
        least = functools.reduce(jnp.minimum, counts)
        need.append((8 - least, most))
    choice = jnp.full((), len(VARIANTS) - 1, jnp.int32)
    for index in reversed(range(len(VARIANTS) - 1)):
        split, cap1, cap2 = VARIANTS[index]
        fits = (need[split][0] <= cap1) & (need[split][1] <= cap2)
        choice = jnp.where(fits, index, choice)
    choice_ref[0] = choice


def layer_kernel(split, cap1, cap2, *refs):
    (
        dest_ref,
        slot_ref,
        req_ref,
        fill_ref,
        q_ref,
        nk_ref,
        nv_ref,
        signs_ref,
        w_ref,
        ck_ref,
        cv_ref,
        out_ref,
        table_ref,
        rk_ref,
        rv_ref,
        plan_vmem,
        plan_ref,
        kc,
        vc,
        first_send,
        mid_k0,
        mid_k1,
        mid_v0,
        mid_v1,
        second_send,
        scores,
        qf,
        part_send,
        pair_recv,
        part_recv,
        att,
        proj,
        load_sem,
        plan_sem,
        first_s,
        first_r,
        second_s,
        second_r,
        pair_s,
        pair_r,
        share_s,
        share_r,
        part_s,
        part_r,
        att_s,
        att_r,
        proj_s,
        proj_r,
    ) = refs
    me = lax.axis_index("inst")
    head = lax.axis_index("head")
    chip, core = me // 2, me % 2
    u, v, _ = coordinates(me, split)
    scale = 1.0 / math.sqrt(HD)
    caches = (kc, vc)
    mids = ((mid_k0, mid_k1), (mid_v0, mid_v1))
    lands = (rk_ref, rv_ref)

    load_k = pltpu.make_async_copy(ck_ref, kc, load_sem.at[0])
    load_v = pltpu.make_async_copy(cv_ref, vc, load_sem.at[1])
    load_k.start()
    load_v.start()

    barrier = pltpu.get_barrier_semaphore()

    def greet(inst):
        pl.semaphore_signal(barrier, inc=1, device_id=(inst, head), device_id_type=MESH)

    def greet_groups(t, _):
        d, j = 1 + t // 2, t % 2
        greet(instance(jnp.bitwise_xor(u, d), v, j, split))
        greet(instance(u, jnp.bitwise_xor(v, d), j, split))
        return 0

    def greet_far(t, _):
        far = instance(jnp.bitwise_xor(u, 1 + t // 3), jnp.bitwise_xor(v, 1 + t % 3), 0, split)
        greet(far)
        return 0

    def greet_head(o, _):
        pl.semaphore_signal(
            barrier, inc=1, device_id=(me, lax.rem(head + o, HEADS)), device_id_type=MESH
        )
        return 0

    lax.fori_loop(1, HEADS, greet_head, 0)
    lax.fori_loop(0, 6, greet_groups, 0)
    greet(chip * 2 + 1 - core)

    @pl.when(core == 0)
    def _():
        lax.fori_loop(0, 9, greet_far, 0)


    write_plan(split, me, dest_ref, req_ref, fill_ref, plan_vmem)
    to_smem = pltpu.make_async_copy(plan_vmem, plan_ref, plan_sem)
    to_smem.start()

    sign_row = (2 * signs_ref[...] - 1).astype(jnp.float32)
    rotate = hadamard(HD)
    raw = q_ref[...].astype(jnp.float32)
    qf[...] = raw
    q_rot = jnp.dot(
        (raw * sign_row).astype(jnp.bfloat16),
        rotate.astype(jnp.bfloat16),
        preferred_element_type=jnp.float32,
    ) * (1.0 / math.sqrt(HD))
    q_low = q_rot.astype(jnp.bfloat16)

    to_smem.wait()
    load_k.wait()
    load_v.wait()
    pl.semaphore_wait(barrier, 13 + HEADS - 1 + 9 * (1 - core))

    def peer(plane, along_first, d, j):
        if (plane == 0) == along_first:
            return instance(jnp.bitwise_xor(u, d), v, j, split)
        return instance(u, jnp.bitwise_xor(v, d), j, split)

    def first_copy(plane, half, d, j):
        src = first_send.at[plane, half, d * 2 + j]
        dst = mids[plane][half].at[pl.ds((d * 2 + core) * GROUP, cap1)]
        sems = first_s.at[plane, half, d * 2 + j], first_r.at[plane, half, d * 2 + core]
        return remote(src, dst, *sems, peer(plane, True, d, j), head)

    def first_keep(plane, half):
        return pltpu.make_async_copy(
            first_send.at[plane, half, core],
            mids[plane][half].at[pl.ds(core * GROUP, cap1)],
            first_r.at[plane, half, core],
        )

    def first_wait(plane, half, d, j):
        dst = mids[plane][half].at[pl.ds((d * 2 + j) * GROUP, cap1)]
        return pltpu.make_async_copy(dst, dst, first_r.at[plane, half, d * 2 + j])

    def second_copy(plane, half, d, j):
        src = second_send.at[plane, half, d * 2 + j]
        dst = lands[plane].at[pl.ds((half * 8 + d * 2 + core) * GROUP, cap2)]
        sems = second_s.at[plane, half, d * 2 + j], second_r.at[plane, half, d * 2 + core]
        return remote(src, dst, *sems, peer(plane, False, d, j), head)

    def second_keep(plane, half):
        return pltpu.make_async_copy(
            second_send.at[plane, half, core],
            lands[plane].at[pl.ds((half * 8 + core) * GROUP, cap2)],
            second_r.at[plane, half, core],
        )

    def second_wait(plane, half, d, j):
        dst = lands[plane].at[pl.ds((half * 8 + d * 2 + j) * GROUP, cap2)]
        return pltpu.make_async_copy(dst, dst, second_r.at[plane, half, d * 2 + j])

    def start_first(half):
        def body(t, _):
            d, j = 3 - t // 2, t % 2
            for plane in range(2):
                first = jnp.bitwise_xor(u if plane == 0 else v, d)
                for m in range(cap1):
                    b = plan_ref[SEND + plane, first * 32 + m * PER + j * 2 + half]
                    first_send[plane, half, d * 2 + j, m] = caches[plane][b]

                @pl.when((d > 0) | (j != core))
                def _(plane=plane):
                    first_copy(plane, half, d, j).start()

                @pl.when((d == 0) & (j == core))
                def _(plane=plane):
                    first_keep(plane, half).start()

            return 0

        lax.fori_loop(0, 8, body, 0)

    def start_second(half):
        def wait_body(t, _):
            for plane in range(2):
                first_wait(plane, half, t // 2, t % 2).wait()
            return 0

        lax.fori_loop(0, 8, wait_body, 0)

        def body(t, _):
            d, j = 3 - t // 2, t % 2
            for plane in range(2):
                base = plan_ref[DEST + plane, d * 2 + j]
                for n in range(cap2):
                    b = base + plan_ref[SOURCE + plane, n]
                    second_send[plane, half, d * 2 + j, n] = mids[plane][half][b]

                @pl.when((d > 0) | (j != core))
                def _(plane=plane):
                    second_copy(plane, half, d, j).start()

                @pl.when((d == 0) & (j == core))
                def _(plane=plane):
                    second_keep(plane, half).start()

            return 0

        lax.fori_loop(0, 8, body, 0)

    start_first(0)
    start_first(1)

    row_max, row_total, acc = attend(plan_ref, q_low, kc, vc, scores, scale)
    lane = lax.broadcasted_iota(jnp.int32, (ROWS, HD), 1)
    part_send[:, :, :HD] = acc.reshape(16, 8, HD)
    part_send[:, :, HD:] = jnp.where(lane < 64, row_max, row_total).reshape(16, 8, HD)

    sibling = chip * 2 + 1 - core

    def att_copy(t):
        c = lax.rem(chip + t, 16)
        return remote(att.at[chip], att.at[chip], att_s.at[t], att_r.at[chip], 2 * c, head)

    def pair_copy():
        return remote(part_send, pair_recv, pair_s, pair_r, sibling, head)

    def part_copy(t):
        c = lax.rem(chip + t, 16)
        return remote(
            part_send.at[c], part_recv.at[chip], part_s.at[t], part_r.at[chip], 2 * c, head
        )

    @pl.when(core == 1)
    def _():
        pair_copy().start()

    @pl.when(core == 0)
    def _():
        pair_copy().wait_recv()
        part_send[...] = joined_pair(part_send[...], pair_recv[...])

        def start_part(t, _):
            part_copy(t).start()
            return 0

        lax.fori_loop(1, 16, start_part, 0)

    table_ref[...] = arrival_table(split, me, dest_ref[...], slot_ref[...])
    start_second(0)

    @pl.when(core == 0)
    def _():
        part_recv[chip] = part_send[chip]

        def got_part(t, _):
            c = lax.rem(chip + t, 16)
            remote(
                part_send.at[0], part_recv.at[c], part_s.at[0], part_r.at[c], 2 * c, head
            ).wait_recv()
            return 0

        lax.fori_loop(1, 16, got_part, 0)
        q_group = qf[pl.ds(pl.multiple_of(chip * 8, 8), 8)].astype(jnp.bfloat16)
        attended = finish_rows(
            part_recv[...],
            chip,
            q_group,
            nk_ref[...],
            nv_ref[...].astype(jnp.float32),
            sign_row,
            rotate,
            scale,
        )
        att[chip] = attended.astype(jnp.bfloat16).astype(jnp.float32)

        def send_att(t, _):
            att_copy(t).start()
            return 0

        lax.fori_loop(1, 16, send_att, 0)

    start_second(1)

    def share_copy():
        return remote(att, att, share_s, share_r, sibling, head)

    @pl.when(core == 0)
    def _():
        def got_att(t, _):
            c = lax.rem(chip + t, 16)
            remote(att.at[c], att.at[c], att_s.at[0], att_r.at[c], 2 * c, head).wait_recv()
            return 0

        lax.fori_loop(1, 16, got_att, 0)
        share_copy().start()

    @pl.when(core == 1)
    def _():
        share_copy().wait_recv()

    everyone = att[...]
    terms = jnp.zeros((16, 256), jnp.float32)
    for h in range(8):
        terms = terms + jnp.dot(
            everyone[:, h, :].astype(jnp.bfloat16),
            w_ref[h * HD : (h + 1) * HD, :],
            preferred_element_type=jnp.float32,
        )
    proj[head] = terms

    def proj_copy(o):
        return remote(
            proj.at[head],
            proj.at[head],
            proj_s.at[o],
            proj_r.at[head],
            me,
            lax.rem(head + o, HEADS),
        )

    def start_proj(o, _):
        proj_copy(o).start()
        return 0

    def got_proj(o, _):
        z = lax.rem(head + o, HEADS)
        remote(proj.at[z], proj.at[z], proj_s.at[o], proj_r.at[z], me, z).wait_recv()
        return 0

    lax.fori_loop(1, HEADS, start_proj, 0)
    lax.fori_loop(1, HEADS, got_proj, 0)
    out_ref[...] = jnp.sum(proj[...], axis=0)

    def sent_proj(o, _):
        proj_copy(o).wait_send()
        return 0

    lax.fori_loop(1, HEADS, sent_proj, 0)

    @pl.when(core == 1)
    def _():
        pair_copy().wait_send()

    @pl.when(core == 0)
    def _():
        def sent_rows(t, _):
            part_copy(t).wait_send()
            att_copy(t).wait_send()
            return 0

        lax.fori_loop(1, 16, sent_rows, 0)
        share_copy().wait_send()

    def finish(t, _):
        d, j = t // 2, t % 2
        for half in range(2):
            for plane in range(2):

                @pl.when((d > 0) | (j != core))
                def _(plane=plane, half=half):
                    first_copy(plane, half, d, j).wait_send()
                    second_copy(plane, half, d, j).wait_send()

                second_wait(plane, half, d, j).wait()
        return 0

    lax.fori_loop(0, 8, finish, 0)


def layer_call(variant, operands):
    split, cap1, cap2 = VARIANTS[variant]
    vmem = pl.BlockSpec(memory_space=pltpu.VMEM)
    smem = pl.BlockSpec(memory_space=pltpu.SMEM)
    hbm = pl.BlockSpec(memory_space=pl.ANY)
    blocks = jax.ShapeDtypeStruct((2 * 8 * GROUP, BT, HD), jnp.bfloat16)
    dma = pltpu.SemaphoreType.DMA

    def low(*lead):
        return pltpu.VMEM((*lead, BT, HD), jnp.bfloat16)

    return pl.pallas_call(
        functools.partial(layer_kernel, split, cap1, cap2),
        out_shape=(
            jax.ShapeDtypeStruct((16, 256), jnp.float32),
            jax.ShapeDtypeStruct((8, 128), jnp.int32),
            blocks,
            blocks,
        ),
        in_specs=[vmem] * 9 + [hbm, hbm],
        out_specs=(vmem, vmem, hbm, hbm),
        scratch_shapes=[
            pltpu.VMEM((8, 128), jnp.int32),
            pltpu.SMEM((8, 128), jnp.int32),
            low(SLOTS),
            low(SLOTS),
            low(2, 2, 8, cap1),
            low(8 * GROUP),
            low(8 * GROUP),
            low(8 * GROUP),
            low(8 * GROUP),
            low(2, 2, 8, cap2),
            pltpu.VMEM((SLOTS // CHUNK, ROWS, CHUNK * BT), jnp.float32),
            pltpu.VMEM((ROWS, HD), jnp.float32),
            pltpu.VMEM((16, 8, 2 * HD), jnp.float32),
            pltpu.VMEM((16, 8, 2 * HD), jnp.float32),
            pltpu.VMEM((16, 8, 2 * HD), jnp.float32),
            pltpu.VMEM((16, 8, HD), jnp.float32),
            pltpu.VMEM((HEADS, 16, 256), jnp.float32),
            dma((2,)),
            dma,
            dma((2, 2, 8)),
            dma((2, 2, 8)),
            dma((2, 2, 8)),
            dma((2, 2, 8)),
            dma,
            dma,
            dma,
            dma,
            dma((16,)),
            dma((16,)),
            dma((16,)),
            dma((16,)),
            dma((HEADS,)),
            dma((HEADS,)),
        ],
        compiler_params=pltpu.CompilerParams(
            collective_id=variant, has_side_effects=True, vmem_limit_bytes=56 * 2**20
        ),
    )(*operands)


def place_kernel(
    table_ref, proj_ref, rk_ref, rv_ref, out_ref, mk_ref, mv_ref, placed, in_sems, out_sems
):
    lands = ((rk_ref, mk_ref), (rv_ref, mv_ref))
    parts, width = 4, SLOTS // 4

    def store(plane, src_plane, part):
        rows = pl.ds(part * width, width)
        return pltpu.make_async_copy(
            placed.at[src_plane, rows], lands[plane][1].at[rows], out_sems.at[plane, part]
        )

    kept = table_ref[0, 0] >= 0

    @pl.when(kept)
    def _():
        for part in range(parts):

            def fetch(t, _):
                s = part * width + t
                landed = table_ref[0, s]
                for plane, row in enumerate((landed // 128, landed % 128)):
                    pltpu.make_async_copy(
                        lands[plane][0].at[row], placed.at[plane, s], in_sems.at[plane, part]
                    ).start()
                return 0

            lax.fori_loop(0, width, fetch, 0, unroll=4)
        for part in range(parts):
            rows = pl.ds(part * width, width)
            for plane in range(2):
                pltpu.make_async_copy(
                    lands[plane][0].at[rows], placed.at[plane, rows], in_sems.at[plane, part]
                ).wait()
                store(plane, plane, part).start()

    @pl.when(jnp.logical_not(kept))
    def _():
        placed[0, :width] = jnp.zeros((width, BT, HD), jnp.bfloat16)
        for plane in range(2):
            for part in range(parts):
                rows = pl.ds(part * width, width)
                pltpu.make_async_copy(
                    placed.at[0, pl.ds(0, width)], lands[plane][1].at[rows], out_sems.at[plane, part]
                ).start()

    out_ref[...] = proj_ref[...].astype(jnp.bfloat16)
    for plane in range(2):
        for part in range(parts):
            store(plane, plane, part).wait()


def static_groups():
    out = []
    for (a0, a1), (b0, b1) in SPLITS:
        rows = []
        for inst in range(INST):
            x, y = inst // 8, inst // 2 % 4
            code = (x ^ (x // 2)) + 4 * (y ^ (y // 2))
            bits = [code >> b & 1 for b in range(4)]
            rows.append((bits[a0] + 2 * bits[a1], bits[b0] + 2 * bits[b1]))
        out.append(np.array(rows, np.int32).T)
    return np.stack(out)


def shards(
    query,
    new_keys,
    new_values,
    cache_keys,
    cache_values,
    signs,
    block_req,
    block_fill,
    dest_inst,
    new_slot,
    out_weight,
):
    vmem = pl.BlockSpec(memory_space=pltpu.VMEM)
    smem = pl.BlockSpec(memory_space=pltpu.SMEM)
    hbm = pl.BlockSpec(memory_space=pl.ANY)
    choice = pl.pallas_call(
        choose_kernel,
        out_shape=jax.ShapeDtypeStruct((1,), jnp.int32),
        in_specs=[smem],
        out_specs=smem,
    )(dest_inst)[0]
    operands = (
        dest_inst.reshape(16, 128),
        new_slot.reshape(16, 128),
        block_req.reshape(16, 128),
        block_fill.reshape(16, 128),
        query.reshape(ROWS, HD),
        new_keys.reshape(16, HD),
        new_values.reshape(16, HD),
        signs,
        out_weight,
        cache_keys.reshape(SLOTS, BT, HD),
        cache_values.reshape(SLOTS, BT, HD),
    )
    branches = [functools.partial(layer_call, variant) for variant in range(len(VARIANTS))]
    proj, table, got_keys, got_values = lax.switch(choice, branches, operands)
    layer_out, moved_keys, moved_values = pl.pallas_call(
        place_kernel,
        out_shape=(
            jax.ShapeDtypeStruct((16, 256), jnp.bfloat16),
            jax.ShapeDtypeStruct((SLOTS, BT, HD), jnp.bfloat16),
            jax.ShapeDtypeStruct((SLOTS, BT, HD), jnp.bfloat16),
        ),
        in_specs=[smem, vmem, hbm, hbm],
        out_specs=(vmem, hbm, hbm),
        scratch_shapes=[
            pltpu.VMEM((2, SLOTS, BT, HD), jnp.bfloat16),
            pltpu.SemaphoreType.DMA((2, 4)),
            pltpu.SemaphoreType.DMA((2, 4)),
        ],
        compiler_params=pltpu.CompilerParams(vmem_limit_bytes=32 * 2**20),
    )(
        table,
        proj,
        got_keys,
        got_values,
    )
    return (
        layer_out.reshape(2, 8, 256),
        moved_keys.reshape(SLOTS, BT, 1, HD),
        moved_values.reshape(SLOTS, BT, 1, HD),
    )


def solution(mesh):
    placed = (
        P(None, None, "head", None),
        P(None, None, "head", None),
        P(None, None, "head", None),
        P("inst", None, "head", None),
        P("inst", None, "head", None),
        P("head", None),
        P(),
        P(),
        P(),
        P(),
        P("head", "inst"),
    )
    return jax.shard_map(
        shards,
        mesh=mesh,
        in_specs=placed,
        out_specs=(
            P(None, None, "inst"),
            P("inst", None, "head", None),
            P("inst", None, "head", None),
        ),
        check_vma=False,
    )
```
